32 devices in a mesh: narrow: 2 (over x), wide: 16 (over z, y, core).
Axes of the slice: x: 2, y: 2, z: 4, core: 2. Of those that a mesh axis runs over, the one named last changes fastest.
Arguments:
- momentum: float32 [4096, 28672], P('narrow', 'wide'), may hold values from -6 to 6
- gradient: bfloat16 [4096, 28672], P('narrow', 'wide'), may hold values from -6 to 6
- right_basis: float32 [28672, 256], P('wide'), may hold values from -0.03125 to 0.03125
- signs: int32 [4096], replicated, may hold values from -1 to 1, as said below
- select: int32 [384], replicated, may hold values from 0 to 4095, as said below
Outputs:
- momentum_out: float32 [4096, 28672], P('narrow', 'wide')
- basis_out: float32 [28672, 256], P('wide')
- update: bfloat16 [4096, 28672], P('narrow', 'wide')
The draws below stay inside these ranges and needn't reach their ends.
Inputs may be any that keep to these rules, and one draw needn't show every extreme that they name: `signs`: each entry is -1 or 1. `select`: 384 distinct row numbers.
All inputs are finite; a program needn't handle non-finite values.
Results may differ from the reference program's by a relative error of at most 0.001.
Values sent between devices are 32-bit elements; how exact they have to be, the bound alone decides.
No kernel may reach another device: no remote copies, remote signals or barrier semaphores. Data moves between devices by JAX's collectives and lax.ppermute only.
A program may use at most 128 MiB of HBM per device.

```python
import math
import jax
import jax.numpy as jnp
from jax import lax

ROWS = 4096
COLS = 28672
RANK = 256
SKETCH = 384


def draw_signs(key, part):
    return 2 * jax.random.randint(jax.random.fold_in(key, 11), (ROWS,), 0, 2, dtype=jnp.int32) - 1


def draw_select(key, part):
    return jax.random.permutation(jax.random.fold_in(key, 23), ROWS)[:SKETCH].astype(jnp.int32)


def strengthened(drawn, stream_key, source, target, blocks, factor):
    def block_of(dim):
        return (jnp.arange(drawn.shape[dim]) // (drawn.shape[dim] // blocks)).reshape((-1,) + (1,) * (drawn.ndim - 1 - dim))

    near = jax.random.permutation(stream_key, blocks)[block_of(target)]
    second = (block_of(target) + blocks // 2) % blocks
    return jnp.where((block_of(source) == near) | (block_of(source) == second), factor * drawn, drawn)


def block_scale(stream_key, extent, shards, least, high):
    def one(dim, blocks):
        steps = jax.random.uniform(jax.random.fold_in(jax.random.fold_in(stream_key, 6), dim), (blocks,), jnp.float32, least / len(shards), high / len(shards))
        return jnp.repeat(jnp.exp(steps), extent[dim] // blocks).reshape((-1,) + (1,) * (len(extent) - dim - 1))

    loudness = one(*shards[0])
    for cut in shards[1:]:
        loudness = loudness * one(*cut)
    return loudness


def centred(own_key, dims, spread, limit, pieces=(), held_as=jnp.bfloat16):
    values = spread * jax.random.normal(own_key, dims, jnp.float32)
    if pieces:
        values = values * block_scale(own_key, dims, pieces, -0.22, 0.18)
    return jnp.clip(values, -limit, limit).astype(held_as)


def bell_draw_with(rng, shape, deviation, reach, pieces, heavy, held_as=jnp.bfloat16):
    values = deviation * jax.random.normal(rng, shape, jnp.float32)
    if pieces:
        values = values * block_scale(rng, shape, pieces, -0.22, 0.18)
    return jnp.clip(strengthened(values, jax.random.fold_in(rng, 3), *heavy), -reach, reach).astype(held_as)


def setup_inputs(seed: int = 0) -> dict:
    splits = jax.random.split(jax.random.key(seed), 6)
    return {
        "momentum": bell_draw_with(splits[0], (ROWS, COLS), 1.0, 6.0, ((0, 2), (1, 16)), (1, 0, 16, 2.0), jnp.float32),
        "gradient": centred(splits[1], (ROWS, COLS), 1.0, 6.0, ((0, 2), (1, 16))),
        "right_basis": centred(splits[2], (COLS, RANK), COLS ** -0.5, 0.03125, ((0, 16),), jnp.float32),
        "signs": draw_signs(jax.random.fold_in(splits[5], 71), 0),
        "select": draw_select(jax.random.fold_in(splits[5], 71), 0),
    }


decay_mu = 0.95
norm_epsilon = 1e-06

def hadamard_rows(select, sign_part, first_row, row_count):
    columns = first_row + jnp.arange(row_count, dtype=jnp.int32)
    shared_bits = jnp.bitwise_and(select[:, None], columns[None, :])
    parity = jnp.zeros(shared_bits.shape, jnp.int32)
    for bit_index in range(ROWS.bit_length()):
        parity = jnp.bitwise_xor(parity, jnp.bitwise_and(jnp.right_shift(shared_bits, bit_index), 1))
    entries = (1 - 2 * parity).astype(jnp.float32) * sign_part.astype(jnp.float32)[None, :]
    return entries / math.sqrt(SKETCH)

def reference(momentum, gradient, right_basis, signs, select):
    high = lax.Precision.HIGHEST
    summed = momentum + gradient.astype(jnp.float32)
    hadamard = hadamard_rows(select, signs, 0, ROWS)
    left_raw = jnp.dot(summed.astype(jnp.float32), right_basis.astype(jnp.float32), precision=high, preferred_element_type=jnp.float32)
    sketch = jnp.dot(hadamard.astype(jnp.float32), left_raw.astype(jnp.float32), precision=high, preferred_element_type=jnp.float32)
    gram = jnp.dot(sketch.T.astype(jnp.float32), sketch.astype(jnp.float32), precision=high, preferred_element_type=jnp.float32)
    lower_factor = jnp.linalg.cholesky(gram)
    left_basis = jax.scipy.linalg.solve_triangular(lower_factor, left_raw.T, lower=True).T
    right_raw = jnp.dot(summed.T.astype(jnp.float32), left_basis.astype(jnp.float32), precision=high, preferred_element_type=jnp.float32)
    norms = jnp.sqrt(lax.optimization_barrier(jnp.sum(right_raw * right_raw, axis=0)) + norm_epsilon)
    basis_out = right_raw / norms[None, :]
    momentum_out = summed - (1.0 - decay_mu) * jnp.dot(left_basis.astype(jnp.float32), right_raw.T.astype(jnp.float32), precision=high, preferred_element_type=jnp.float32)
    scale_factor = math.sqrt(ROWS * COLS / RANK)
    update = (scale_factor * jnp.dot(left_basis.astype(jnp.float32), basis_out.T.astype(jnp.float32), precision=high, preferred_element_type=jnp.float32)).astype(jnp.bfloat16)
    return (momentum_out, basis_out, update)
```

```python
import functools
import math

import jax
import jax.numpy as jnp
from jax import lax
from jax.experimental import pallas as pl
from jax.experimental.pallas import tpu as pltpu
from jax.sharding import PartitionSpec as P

decay_mu = 0.95
norm_epsilon = 1e-06

F32 = jnp.float32
BF16 = jnp.bfloat16
HIGH = lax.Precision.HIGHEST
MIB = 1024 * 1024


def split2(x):
    hi = x.astype(BF16)
    return hi, (x - hi.astype(F32)).astype(BF16)


def dot(a, b):
    return jnp.dot(a, b, preferred_element_type=F32)


def params(mib):
    return pltpu.CompilerParams(
        vmem_limit_bytes=mib * MIB, dimension_semantics=("arbitrary",)
    )


def cost(flops, bytes_accessed):
    return pl.CostEstimate(
        flops=int(flops), bytes_accessed=int(bytes_accessed), transcendentals=0
    )


def left_kernel(
    blocks,
    info,
    m_ref,
    g_ref,
    b_ref,
    signs_ref,
    select_ref,
    shi_ref,
    slo_ref,
    send1_ref,
    keep1_ref,
    send2_ref,
    keep2_ref,
    skend_ref,
    skkeep_ref,
    bhi,
    blo,
    lt,
    sketch,
):
    step = pl.program_id(0)
    beta = info[0]
    tile = m_ref.shape[0]
    rank = b_ref.shape[1]
    chunk = rank // 2
    groups = chunk // 8

    @pl.when(step == 0)
    def _():
        hi, lo = split2(b_ref[...])
        bhi[...] = hi
        blo[...] = lo
        sketch[...] = jnp.zeros_like(sketch)

    hi, lo = split2(m_ref[...] + g_ref[...].astype(F32))
    shi_ref[...] = hi
    slo_ref[...] = lo
    left = dot(hi, bhi[...]) + (dot(lo, bhi[...]) + dot(hi, blo[...]))
    lt[...] = left.T
    for c, (keep, send) in enumerate(((keep1_ref, send1_ref), (keep2_ref, send2_ref))):
        for p in range(groups):
            start = pl.multiple_of(c * chunk + 8 * (beta ^ p), 8)
            rows = lt[pl.ds(start, 8), :]
            if p < groups // 2:
                keep[8 * p : 8 * p + 8, :] = rows
            else:
                q = p - groups // 2
                send[8 * q : 8 * q + 8, :] = rows

    sketch_rows = select_ref.shape[0]
    column = info[1] + step * tile + lax.broadcasted_iota(jnp.int32, (1, tile), 1)
    bits = jnp.bitwise_and(select_ref[...], column)
    for shift in (8, 4, 2, 1):
        bits = jnp.bitwise_xor(bits, jnp.right_shift(bits, shift))
    bits = jnp.bitwise_and(bits, 1)
    hadamard = ((1 - 2 * bits) * signs_ref[...]).astype(F32).astype(BF16)
    l0, rest = left.astype(BF16), None
    rest = left - l0.astype(F32)
    l1 = rest.astype(BF16)
    l2 = (rest - l1.astype(F32)).astype(BF16)
    sketch[...] += dot(hadamard, l0) + (dot(hadamard, l1) + dot(hadamard, l2))

    @pl.when(step == blocks - 1)
    def _():
        scale = 1.0 / math.sqrt(sketch_rows)
        share = sketch_rows // groups
        for p in range(groups):
            for i in range(share // 8):
                start = pl.multiple_of(share * (beta ^ p) + 8 * i, 8)
                rows = sketch[pl.ds(start, 8), :] * scale
                if p < groups // 2:
                    skkeep_ref[8 * p : 8 * p + 8, rank * i : rank * i + rank] = rows
                else:
                    q = p - groups // 2
                    skend_ref[8 * q : 8 * q + 8, rank * i : rank * i + rank] = rows


def left_call(info, momentum, gradient, right_basis, signs, select):
    rows, cols = momentum.shape
    rank = right_basis.shape[1]
    sketch_rows = select.shape[0]
    tile = 256
    blocks = rows // tile
    quarter = rank // 4
    wide_sketch = sketch_rows // (rank // 16) // 8 * rank
    part = jax.ShapeDtypeStruct((quarter, rows), F32)
    part_spec = pl.BlockSpec((quarter, tile), lambda i, s: (0, i))
    sk = jax.ShapeDtypeStruct((quarter, wide_sketch), F32)
    sk_spec = pl.BlockSpec((quarter, wide_sketch), lambda i, s: (0, 0))
    row_spec = pl.BlockSpec((tile, cols), lambda i, s: (i, 0))
    return pl.pallas_call(
        functools.partial(left_kernel, blocks),
        grid_spec=pltpu.PrefetchScalarGridSpec(
            num_scalar_prefetch=1,
            grid=(blocks,),
            in_specs=[
                row_spec,
                row_spec,
                pl.BlockSpec((cols, rank), lambda i, s: (0, 0)),
                pl.BlockSpec((1, tile), lambda i, s: (0, s[1] // tile + i)),
                pl.BlockSpec((sketch_rows, 1), lambda i, s: (0, 0)),
            ],
            out_specs=[row_spec, row_spec] + [part_spec] * 4 + [sk_spec] * 2,
            scratch_shapes=[
                pltpu.VMEM((cols, rank), BF16),
                pltpu.VMEM((cols, rank), BF16),
                pltpu.VMEM((rank, tile), F32),
                pltpu.VMEM((sketch_rows, rank), F32),
            ],
        ),
        out_shape=[
            jax.ShapeDtypeStruct((rows, cols), BF16),
            jax.ShapeDtypeStruct((rows, cols), BF16),
            part,
            part,
            part,
            part,
            sk,
            sk,
        ],
        compiler_params=params(40),
        cost_estimate=cost(6 * rows * cols * rank, rows * cols * 10),
        name="left_factor",
    )(info, momentum, gradient, right_basis, signs[None, :], select[:, None])


def right_kernel(a_ref, b_ref, shi_ref, slo_ref, w_ref):
    step = pl.program_id(0)
    left = jnp.concatenate([a_ref[...], b_ref[...]], axis=0)
    hi, lo = split2(left)
    half = left.shape[0]
    both = dot(jnp.concatenate([hi, lo], axis=0), shi_ref[...])
    term = (both[:half] + both[half:]) + dot(hi, slo_ref[...])

    @pl.when(step == 0)
    def _():
        w_ref[...] = term

    @pl.when(step > 0)
    def _():
        w_ref[...] += term


def right_call(first, second, shi, slo):
    rows, cols = shi.shape
    quarter = first.shape[0]
    tile = 256
    part_spec = pl.BlockSpec((quarter, tile), lambda i: (0, i))
    row_spec = pl.BlockSpec((tile, cols), lambda i: (i, 0))
    return pl.pallas_call(
        right_kernel,
        grid=(rows // tile,),
        in_specs=[part_spec, part_spec, row_spec, row_spec],
        out_specs=pl.BlockSpec((2 * quarter, cols), lambda i: (0, 0)),
        out_shape=jax.ShapeDtypeStruct((2 * quarter, cols), F32),
        compiler_params=params(30),
        cost_estimate=cost(12 * rows * cols * quarter, rows * cols * 4),
        name="right_factor",
    )(first, second, shi, slo)


def eliminate(block):
    n = block.shape[0]
    row_id = lax.broadcasted_iota(jnp.int32, (n, n), 0)
    lane_id = lax.broadcasted_iota(jnp.int32, (n, n), 1)
    groups = [block[8 * g : 8 * g + 8, :] for g in range(n // 8)]
    lane = lane_id[:8, :]
    sub = row_id[:8, :]
    for k in range(n):
        g0 = k // 8
        row = groups[g0][k % 8 : k % 8 + 1, :]
        inverse = 1.0 / row[:, k : k + 1]
        scaled = row * inverse
        scaled = jnp.broadcast_to(scaled, (8, n))
        is_pivot = lane == k
        inverse = jnp.broadcast_to(inverse, (8, n))
        for g in range(g0, n // 8):
            x = groups[g]
            col = x[:, k : k + 1]
            if g == g0:
                col = jnp.where(sub[:, :1] > k % 8, col, 0.0)
                keep = jnp.logical_and(is_pivot, sub > k % 8)
            else:
                keep = is_pivot
            groups[g] = jnp.where(keep, -(col * inverse), x - col * scaled)
    full = jnp.concatenate(groups, axis=0)
    diagonal = jnp.sum(jnp.where(row_id == lane_id, full, 0.0), axis=1, keepdims=True)
    unit = jnp.where(row_id > lane_id, full, jnp.where(row_id == lane_id, 1.0, 0.0))
    return unit * lax.rsqrt(diagonal)


def dot_high(a, b, dims=((1,), (0,))):
    return lax.dot_general(
        a, b, (dims, ((), ())), precision=HIGH, preferred_element_type=F32
    )


def factor_kernel(info, *refs):
    parts, (hi_ref, lo_ref) = refs[:-2], refs[-2:]
    gram = None
    for ref in parts:
        term = dot_high(ref[...], ref[...], ((0,), (0,)))
        gram = term if gram is None else gram + term
    rank = gram.shape[0]
    half = rank // 2
    a21 = gram[half:, :half]
    inv11 = eliminate(gram[:half, :half])
    l21 = dot_high(a21, inv11, ((1,), (1,)))
    inv22 = eliminate(gram[half:, half:] - dot_high(l21, l21, ((1,), (1,))))
    inv21 = -dot_high(inv22, dot_high(l21, inv11))
    top = jnp.concatenate([inv11, jnp.zeros_like(inv11)], axis=1)
    inverse = jnp.concatenate([top, jnp.concatenate([inv21, inv22], axis=1)], axis=0)
    source = lax.broadcasted_iota(jnp.int32, (rank, rank), 0)
    target = lax.broadcasted_iota(jnp.int32, (rank, rank), 1)
    order = jnp.where(source == jnp.bitwise_xor(target, 8 * info[0]), 1.0, 0.0)
    hi, lo = split2(dot_high(inverse, order.astype(F32)))
    hi_ref[...] = hi
    lo_ref[...] = lo


def factor_call(info, sk_first, sk_second, rank):
    quarter, lanes = sk_first.shape
    specs = [
        pl.BlockSpec((quarter, rank), functools.partial(lambda j, i, s: (0, j), j))
        for j in range(lanes // rank)
    ]
    out = jax.ShapeDtypeStruct((rank, rank), BF16)
    out_spec = pl.BlockSpec((rank, rank), lambda i, s: (0, 0))
    return pl.pallas_call(
        factor_kernel,
        grid_spec=pltpu.PrefetchScalarGridSpec(
            num_scalar_prefetch=1,
            grid=(1,),
            in_specs=specs + specs,
            out_specs=[out_spec, out_spec],
        ),
        out_shape=[out, out],
        compiler_params=params(30),
        cost_estimate=cost(2e10, 1e6),
        name="factor_inverse",
    )(info, *([sk_first] * len(specs) + [sk_second] * len(specs)))


def basis_kernel(hi_ref, lo_ref, a_ref, b_ref, c_ref, d_ref, lhi_ref, llo_ref):
    raw = jnp.concatenate([a_ref[...], b_ref[...], c_ref[...], d_ref[...]], axis=0)
    hi, lo = split2(raw)
    basis = dot(hi_ref[...], hi) + (dot(hi_ref[...], lo) + dot(lo_ref[...], hi))
    hi, lo = split2(basis.T)
    lhi_ref[...] = hi
    llo_ref[...] = lo


def basis_call(inv, parts):
    quarter, rows = parts[0].shape
    rank = inv[0].shape[0]
    tile = 256
    inv_spec = pl.BlockSpec((rank, rank), lambda i: (0, 0))
    part_spec = pl.BlockSpec((quarter, tile), lambda i: (0, i))
    out_spec = pl.BlockSpec((tile, rank), lambda i: (i, 0))
    out = jax.ShapeDtypeStruct((rows, rank), BF16)
    return pl.pallas_call(
        basis_kernel,
        grid=(rows // tile,),
        in_specs=[inv_spec] * 2 + [part_spec] * 4,
        out_specs=[out_spec] * 2,
        out_shape=[out, out],
        compiler_params=params(20),
        cost_estimate=cost(6 * rows * rank * rank, rows * rank * 8),
        name="left_basis",
    )(*inv, *parts)


def rotate_kernel(hi_ref, lo_ref, *refs):
    parts, (r_ref, rhi_ref, rlo_ref, squares_ref) = refs[:-4], refs[-4:]
    per = len(parts) // 2
    halves = []
    for c in range(2):
        total = parts[c * per][...]
        for ref in parts[c * per + 1 : (c + 1) * per]:
            total = total + ref[...]
        halves.append(total)
    hi, lo = split2(jnp.concatenate(halves, axis=0))
    right = dot(hi_ref[...], hi) + (dot(hi_ref[...], lo) + dot(lo_ref[...], hi))
    r_ref[...] = right
    hi, lo = split2((1.0 - decay_mu) * right)
    rhi_ref[...] = hi
    rlo_ref[...] = lo
    squares = jnp.sum(right * right, axis=1, keepdims=True)
    squares_ref[...] = jnp.broadcast_to(squares, (right.shape[0], 128)).T[:8, :]


def rotate_call(inv, parts):
    half, cols = parts[0].shape
    rank = 2 * half
    return pl.pallas_call(
        rotate_kernel,
        out_shape=[
            jax.ShapeDtypeStruct((rank, cols), F32),
            jax.ShapeDtypeStruct((rank, cols), BF16),
            jax.ShapeDtypeStruct((rank, cols), BF16),
            jax.ShapeDtypeStruct((8, rank), F32),
        ],
        compiler_params=pltpu.CompilerParams(vmem_limit_bytes=40 * MIB),
        cost_estimate=cost(6 * cols * rank * rank, cols * rank * 16),
        name="right_rotate",
    )(*inv, *parts)


def momentum_kernel(shi_ref, slo_ref, lhi_ref, llo_ref, rhi_ref, rlo_ref, out_ref):
    lhi = lhi_ref[...]
    term = dot(lhi, rhi_ref[...]) + (dot(lhi, rlo_ref[...]) + dot(llo_ref[...], rhi_ref[...]))
    out_ref[...] = (shi_ref[...].astype(F32) + slo_ref[...].astype(F32)) - term


def momentum_call(shi, slo, left, right):
    rows, cols = shi.shape
    rank = right[0].shape[0]
    tile = 256
    row_spec = pl.BlockSpec((tile, cols), lambda i: (i, 0))
    left_spec = pl.BlockSpec((tile, rank), lambda i: (i, 0))
    right_spec = pl.BlockSpec((rank, cols), lambda i: (0, 0))
    return pl.pallas_call(
        momentum_kernel,
        grid=(rows // tile,),
        in_specs=[row_spec] * 2 + [left_spec] * 2 + [right_spec] * 2,
        out_specs=row_spec,
        out_shape=jax.ShapeDtypeStruct((rows, cols), F32),
        compiler_params=params(40),
        cost_estimate=cost(6 * rows * cols * rank, rows * cols * 8),
        name="momentum_update",
    )(shi, slo, *left, *right)


def update_kernel(factor, r_ref, squares_ref, lhi_ref, llo_ref, update_ref, basis_ref, bhi, blo):
    @pl.when(pl.program_id(0) == 0)
    def _():
        rank = r_ref.shape[0]
        squares = jnp.broadcast_to(squares_ref[:1, :], (128, rank)).T[:, :1]
        basis = r_ref[...] / jnp.sqrt(squares + norm_epsilon)
        basis_ref[...] = basis.T
        hi, lo = split2(factor * basis)
        bhi[...] = hi
        blo[...] = lo

    lhi = lhi_ref[...]
    term = dot(lhi, bhi[...]) + (dot(lhi, blo[...]) + dot(llo_ref[...], bhi[...]))
    update_ref[...] = term.astype(BF16)


def update_call(factor, right, squares, left):
    rank, cols = right.shape
    rows = left[0].shape[0]
    tile = 256
    left_spec = pl.BlockSpec((tile, rank), lambda i: (i, 0))
    return pl.pallas_call(
        functools.partial(update_kernel, factor),
        grid=(rows // tile,),
        in_specs=[
            pl.BlockSpec((rank, cols), lambda i: (0, 0)),
            pl.BlockSpec((8, rank), lambda i: (0, 0)),
            left_spec,
            left_spec,
        ],
        out_specs=[
            pl.BlockSpec((tile, cols), lambda i: (i, 0)),
            pl.BlockSpec((cols, rank), lambda i: (0, 0)),
        ],
        out_shape=[
            jax.ShapeDtypeStruct((rows, cols), BF16),
            jax.ShapeDtypeStruct((cols, rank), F32),
        ],
        scratch_shapes=[pltpu.VMEM((rank, cols), BF16), pltpu.VMEM((rank, cols), BF16)],
        compiler_params=params(40),
        cost_estimate=cost(6 * rows * cols * rank, rows * cols * 2),
        name="update_basis",
    )(right, squares, *left)


def swap(x, axis, size, bit):
    return lax.ppermute(x, axis, [(i, i ^ bit) for i in range(size)])


def scatter_sum(wide, keep, send):
    got = swap(send, "wide", wide, 1)
    h = keep.shape[0] // 2
    send = keep[h:] + got[h:]
    keep = keep[:h] + got[:h]
    got = swap(send, "wide", wide, 2)
    total = keep + got
    q = h // 4
    mine = total[:q]
    got = [swap(total[q * d : q * d + q], "wide", wide, 4 * d) for d in (1, 2, 3)]
    return mine + (got[0] + got[1] + got[2])


def gather_parts(wide, mine):
    got = [swap(mine, "wide", wide, 4 * d) for d in (1, 2, 3)]
    quad = jnp.concatenate([mine] + got, axis=0)
    half = jnp.concatenate([quad, swap(quad, "wide", wide, 2)], axis=0)
    return half, swap(half, "wide", wide, 1)


def per_device(narrow, wide, whole_rows, whole_cols, momentum, gradient, right_basis, signs, select):
    rows, cols = momentum.shape
    rank = right_basis.shape[1]
    fast = narrow == 2 and wide == 16
    narrow_index = lax.axis_index("narrow")
    index = lax.axis_index("wide")
    if fast:
        core, y, z = index % 2, (index // 2) % 2, index // 4
        beta = 8 * core + 4 * y + z
    else:
        beta = index * 0
    info = jnp.stack([beta, narrow_index * rows]).astype(jnp.int32)
    shi, slo, send1, keep1, send2, keep2, sk_send, sk_keep = left_call(
        info, momentum, gradient, right_basis, signs, select
    )
    if fast:
        mine1 = scatter_sum(wide, keep1, send1)
        first1, second1 = gather_parts(wide, mine1)
        mine_sk = scatter_sum(wide, sk_keep, sk_send)
        mine_sk = mine_sk + swap(mine_sk, "narrow", narrow, 1)
        sk_first, sk_second = gather_parts(wide, mine_sk)
        mine2 = scatter_sum(wide, keep2, send2)
        first2, second2 = gather_parts(wide, mine2)
    else:
        first1, second1, first2, second2 = lax.psum((keep1, send1, keep2, send2), "wide")
        sk_first, sk_second = lax.psum((sk_keep, sk_send), ("narrow", "wide"))
    w1 = right_call(first1, second1, shi, slo)
    w2 = right_call(first2, second2, shi, slo)
    if fast:
        parts = [w1, swap(w1, "narrow", narrow, 1), w2, swap(w2, "narrow", narrow, 1)]
    else:
        parts = list(lax.psum((w1, w2), "narrow"))
    inv = factor_call(info, sk_first, sk_second, rank)
    left = basis_call(inv, [first1, second1, first2, second2])
    right, rhi, rlo, squares = rotate_call(inv, parts)
    if fast:
        for bit in (1, 2, 4, 8):
            squares = squares + swap(squares, "wide", wide, bit)
    else:
        squares = lax.psum(squares, "wide")
    momentum_out = momentum_call(shi, slo, left, (rhi, rlo))
    factor = math.sqrt(whole_rows * whole_cols / rank)
    update, basis_out = update_call(factor, right, squares, left)
    return momentum_out, basis_out, update


def solution(mesh):
    in_specs = (P("narrow", "wide"), P("narrow", "wide"), P("wide", None), P(), P())
    out_specs = (P("narrow", "wide"), P("wide", None), P("narrow", "wide"))
    narrow, wide = mesh.shape["narrow"], mesh.shape["wide"]

    def whole(momentum, *rest):
        body = functools.partial(per_device, narrow, wide, *momentum.shape)
        return jax.shard_map(
            body, mesh=mesh, in_specs=in_specs, out_specs=out_specs, check_vma=False
        )(momentum, *rest)

    return whole
```

```python
import functools
import math

import jax
import jax.numpy as jnp
from jax import lax
from jax.experimental import pallas as pl
from jax.experimental.pallas import tpu as pltpu
from jax.sharding import PartitionSpec as P

decay_mu = 0.95
norm_epsilon = 1e-06

F32 = jnp.float32
BF16 = jnp.bfloat16
HIGH = lax.Precision.HIGHEST
MIB = 1024 * 1024
WHOLE = pl.BlockSpec(memory_space=pltpu.VMEM)


def split2(x):
    hi = x.astype(BF16)
    return hi, (x - hi.astype(F32)).astype(BF16)


def dot(a, b):
    return jnp.dot(a, b, preferred_element_type=F32)


in_space = pltpu.with_memory_space_constraint


def params(mib):
    return pltpu.CompilerParams(
        vmem_limit_bytes=mib * MIB, dimension_semantics=("arbitrary",)
    )


def cost(flops, bytes_accessed):
    return pl.CostEstimate(
        flops=int(flops), bytes_accessed=int(bytes_accessed), transcendentals=0
    )


TILE = 512
SLOTS = 2


def is_fast(narrow, wide):
    return narrow == 2 and wide == 16


def labels_of(fast):
    if not fast:
        return 0, 4
    index = lax.axis_index("wide")
    core, y, z = index & 1, (index >> 1) & 1, index >> 2
    za = (z >> 1) ^ (z & 1)
    even, odd = 2 * y + za, 4 + 2 * za + y
    return even + core * (odd - even), odd + core * (even - odd)


def left_kernel(
    fast,
    m_hbm,
    g_hbm,
    b_hbm,
    shi_ref,
    slo_ref,
    send_ref,
    keep_ref,
    m_ref,
    g_ref,
    b_ref,
    bhi,
    blo,
    lt,
    sems,
    b_sem,
):
    rows, cols = m_hbm.shape
    rank = b_ref.shape[1]
    block = rank // 8
    tiles = rows // TILE
    labels = labels_of(fast)

    def copies(t):
        source, slot = pl.ds(t * TILE, TILE), pl.ds(t % SLOTS * TILE, TILE)
        return (
            pltpu.make_async_copy(m_hbm.at[source], m_ref.at[slot], sems.at[0, t % SLOTS]),
            pltpu.make_async_copy(g_hbm.at[source], g_ref.at[slot], sems.at[1, t % SLOTS]),
        )

    b_copy = pltpu.make_async_copy(b_hbm, b_ref, b_sem)
    b_copy.start()
    for t in range(min(SLOTS - 1, tiles)):
        for copy in copies(t):
            copy.start()
    b_copy.wait()
    bhi[...], blo[...] = split2(b_ref[...])

    for t in range(tiles):
        for copy in copies(t):
            copy.wait()
        if t + SLOTS - 1 < tiles:
            for copy in copies(t + SLOTS - 1):
                copy.start()
        part, slot = slice(t * TILE, t * TILE + TILE), t % SLOTS * TILE
        slot = slice(slot, slot + TILE)
        hi, lo = split2(m_ref[slot, :] + g_ref[slot, :].astype(F32))
        shi_ref[part, :] = hi
        slo_ref[part, :] = lo
        left = dot(hi, bhi[...]) + (dot(lo, bhi[...]) + dot(hi, blo[...]))
        lt[...] = left.T
        for side, ref in enumerate((keep_ref, send_ref)):
            for q in range(4):
                start = pl.multiple_of(block * (labels[side] ^ q), block)
                ref[block * q : block * q + block, part] = lt[pl.ds(start, block), :]


def left_call(fast, momentum, gradient, right_basis):
    rows, cols = momentum.shape
    rank = right_basis.shape[1]
    part = jax.ShapeDtypeStruct((rank // 2, rows), F32)
    hbm = pl.BlockSpec(memory_space=pltpu.HBM)
    return pl.pallas_call(
        functools.partial(left_kernel, fast),
        in_specs=[hbm] * 3,
        out_specs=[WHOLE] * 4,
        out_shape=[
            pltpu.VMEM((rows, cols), BF16),
            pltpu.VMEM((rows, cols), BF16),
            part,
            part,
        ],
        scratch_shapes=[
            pltpu.VMEM((SLOTS * TILE, cols), F32),
            pltpu.VMEM((SLOTS * TILE, cols), BF16),
            pltpu.VMEM((cols, rank), F32),
            pltpu.VMEM((cols, rank), BF16),
            pltpu.VMEM((cols, rank), BF16),
            pltpu.VMEM((rank, TILE), F32),
            pltpu.SemaphoreType.DMA((2, SLOTS)),
            pltpu.SemaphoreType.DMA,
        ],
        compiler_params=pltpu.CompilerParams(vmem_limit_bytes=24 * MIB),
        cost_estimate=cost(6 * rows * cols * rank, rows * cols * 6),
        name="left_factor",
    )(*(in_space(x, pltpu.HBM) for x in (momentum, gradient, right_basis)))


def sketch_kernel(fast, scale, a_ref, b_ref, select_ref, signs_ref, *refs):
    left_ref, sketch_ref = refs[-2:]
    half, rows = a_ref.shape
    rank = 2 * half
    block = rank // 8
    labels = labels_of(fast)
    for side, ref in enumerate((a_ref, b_ref)):
        for q in range(4):
            start = pl.multiple_of(block * (labels[side] ^ q), block)
            hi, lo = split2(ref[block * q : block * q + block, :])
            left_ref[pl.ds(start, block), :] = hi
            left_ref[pl.ds(pl.multiple_of(rank + start, block), block), :] = lo
    first = pl.multiple_of(lax.axis_index("narrow") * rows, rows)
    column = first + lax.broadcasted_iota(jnp.int32, (1, rows), 1)
    bits = jnp.bitwise_and(select_ref[...], column)
    for shift in (8, 4, 2, 1):
        bits = jnp.bitwise_xor(bits, jnp.right_shift(bits, shift))
    entries = (1 - 2 * jnp.bitwise_and(bits, 1)) * signs_ref[:, pl.ds(first, rows)]
    both = lax.dot_general(
        entries.astype(F32).astype(BF16),
        left_ref[...],
        (((1,), (1,)), ((), ())),
        preferred_element_type=F32,
    )
    sketch_ref[...] = (both[:, :rank] + both[:, rank:]) * scale


def sketch_call(fast, first, second, select, signs, scale, held):
    half, rows = first.shape
    rank = 2 * half
    return pl.pallas_call(
        functools.partial(sketch_kernel, fast, scale),
        in_specs=[WHOLE] * (4 + len(held)),
        out_specs=[WHOLE] * 2,
        out_shape=[
            jax.ShapeDtypeStruct((2 * rank, rows), BF16),
            jax.ShapeDtypeStruct((select.shape[0], rank), F32),
        ],
        compiler_params=pltpu.CompilerParams(vmem_limit_bytes=24 * MIB),
        cost_estimate=cost(4 * select.shape[0] * rank * rows, rows * rank * 8),
        name="sketch_rows",
    )(
        first,
        second,
        select[:, None],
        signs[None, :],
        *(in_space(x, pltpu.VMEM) for x in held),
    )


def right_kernel(first, left_ref, shi_ref, slo_ref, *refs):
    if len(refs) > 1:
        mine_ref, other_ref, w_ref, sketch_ref = refs
        sketch_ref[...] = mine_ref[...] + other_ref[...]
    else:
        (w_ref,) = refs
    rank, cols = w_ref.shape
    for start in range(0, cols, 256):
        stop = min(start + 256, cols)
        source = slice(first + start, first + stop)
        both = dot(left_ref[...], shi_ref[:, source])
        last = dot(left_ref[:rank, :], slo_ref[:, source])
        w_ref[:, start:stop] = (both[:rank] + both[rank:]) + last


def right_call(left, shi, slo, first, stop, *sketches):
    rows = shi.shape[0]
    rank = left.shape[0] // 2
    cols = stop - first
    outs = [jax.ShapeDtypeStruct((rank, cols), F32)]
    if sketches:
        outs.append(jax.ShapeDtypeStruct(sketches[0].shape, F32))
    return pl.pallas_call(
        functools.partial(right_kernel, first),
        in_specs=[WHOLE] * (3 + len(sketches)),
        out_specs=[WHOLE] * len(outs),
        out_shape=outs,
        compiler_params=pltpu.CompilerParams(vmem_limit_bytes=24 * MIB),
        cost_estimate=cost(6 * rows * cols * rank, rows * cols * 4),
        name="right_factor",
    )(left, in_space(shi, pltpu.VMEM), in_space(slo, pltpu.VMEM), *sketches)


def eliminate(block):
    n = block.shape[0]
    groups = [block[8 * g : 8 * g + 8, :] for g in range(n // 8)]
    lane = lax.broadcasted_iota(jnp.int32, (8, n), 1)
    out = []
    for k in range(0, n, 4):
        g0, o = k // 8, k % 8
        rows = [groups[g0][o + j : o + j + 1, :] for j in range(4)]

        def entry(i, j):
            return jnp.broadcast_to(rows[i][:, k + j : k + j + 1], (8, n))

        u = [[entry(i, j) if j >= i else None for j in range(4)] for i in range(4)]
        inv = []
        low = [[None] * 4 for _ in range(4)]
        for i in range(4):
            inv.append(1.0 / u[i][i])
            for r in range(i + 1, 4):
                low[r][i] = u[i][r] * inv[i]
                for j in range(r, 4):
                    u[r][j] = u[r][j] - low[r][i] * u[i][j]
        inside = jnp.logical_and(lane >= k, lane < k + 4)
        q = []
        for i in range(4):
            base = jnp.where(inside, 0.0, jnp.broadcast_to(rows[i], (8, n)))
            base = jnp.where(lane == k + i, 1.0, base)
            for j in range(i):
                base = base - low[i][j] * q[j]
            q.append(base)
            out.append(jnp.where(lane <= k + i, base * lax.rsqrt(u[i][i]), 0.0)[:1])
        for g in range(g0 if o == 0 else g0 + 1, n // 8):
            x = groups[g]
            new = jnp.where(inside, 0.0, x)
            h = []
            for i in range(4):
                c = jnp.broadcast_to(x[:, k + i : k + i + 1], (8, n))
                for j in range(i):
                    c = c - h[j] * u[j][i]
                h.append(c * inv[i])
                new = new - h[i] * q[i]
            groups[g] = new
    return jnp.concatenate(out, axis=0)


def dot_high(a, b, dims=((1,), (0,))):
    return lax.dot_general(
        a, b, (dims, ((), ())), precision=HIGH, preferred_element_type=F32
    )


def factor_kernel(a_ref, b_ref, hi_ref, lo_ref):
    sketch = jnp.concatenate([a_ref[...], b_ref[...]], axis=0)
    gram = dot_high(sketch, sketch, ((0,), (0,)))
    half = gram.shape[0] // 2
    inv11 = eliminate(gram[:half, :half])
    l21 = dot_high(gram[half:, :half], inv11, ((1,), (1,)))
    inv22 = eliminate(gram[half:, half:] - dot_high(l21, l21, ((1,), (1,))))
    inv21 = -dot_high(inv22, dot_high(l21, inv11))
    top = jnp.concatenate([inv11, jnp.zeros_like(inv11)], axis=1)
    inverse = jnp.concatenate([top, jnp.concatenate([inv21, inv22], axis=1)], axis=0)
    hi_ref[...], lo_ref[...] = split2(inverse)


def factor_call(first, second):
    rank = first.shape[1]
    out = jax.ShapeDtypeStruct((rank, rank), BF16)
    return pl.pallas_call(
        factor_kernel,
        in_specs=[WHOLE] * 2,
        out_specs=[WHOLE] * 2,
        out_shape=[out, out],
        compiler_params=pltpu.CompilerParams(vmem_limit_bytes=24 * MIB),
        cost_estimate=cost(1e6, 1e5),
        name="factor_inverse",
    )(first, second)


def basis_kernel(hi_ref, lo_ref, raw_ref, terms_ref, basis_ref):
    rank = hi_ref.shape[0]
    hi, lo = raw_ref[:rank, :], raw_ref[rank:, :]
    basis = dot(hi_ref[...], hi) + (dot(hi_ref[...], lo) + dot(lo_ref[...], hi))
    basis = basis.T
    basis_ref[...] = basis
    hi, lo = split2(basis)
    terms_ref[...] = jnp.concatenate([hi, lo, hi], axis=1)


def basis_call(inv, raw):
    rows = raw.shape[1]
    rank = inv[0].shape[0]
    tile = 256
    inv_spec = pl.BlockSpec((rank, rank), lambda i: (0, 0))
    return pl.pallas_call(
        basis_kernel,
        grid=(rows // tile,),
        in_specs=[inv_spec] * 2 + [pl.BlockSpec((2 * rank, tile), lambda i: (0, i))],
        out_specs=[
            pl.BlockSpec((tile, 3 * rank), lambda i: (i, 0)),
            pl.BlockSpec((tile, rank), lambda i: (i, 0)),
        ],
        out_shape=[
            jax.ShapeDtypeStruct((rows, 3 * rank), BF16),
            jax.ShapeDtypeStruct((rows, rank), F32),
        ],
        compiler_params=params(24),
        cost_estimate=cost(1e6, 1e5),
        name="left_basis",
    )(*inv, raw)


def rotate_kernel(pieces, hi_ref, lo_ref, *refs):
    parts, (turned_ref, terms_ref, squares_ref) = refs[:-3], refs[-3:]
    rank = hi_ref.shape[0]
    squares = jnp.zeros((rank, 1), F32)
    start = 0
    for piece in pieces:
        total = piece[0]
        total = parts[total][...]
        for other in piece[1:]:
            total = total + parts[other][...]
        stop = start + total.shape[1]
        hi, lo = split2(total)
        right = dot(hi_ref[...], hi) + (dot(hi_ref[...], lo) + dot(lo_ref[...], hi))
        turned_ref[start:stop, :] = right.T
        hi, lo = split2((1.0 - decay_mu) * right)
        terms_ref[:rank, start:stop] = hi
        terms_ref[rank : 2 * rank, start:stop] = hi
        terms_ref[2 * rank :, start:stop] = lo
        squares = squares + jnp.sum(right * right, axis=1, keepdims=True)
        start = stop
    squares_ref[...] = jnp.broadcast_to(squares, (rank, 128)).T[:8, :]


def rotate_call(inv, pieces):
    rank = inv[0].shape[0]
    cols = sum(piece[0].shape[1] for piece in pieces)
    flat, places = [], []
    for piece in pieces:
        places.append(tuple(range(len(flat), len(flat) + len(piece))))
        flat.extend(piece)
    return pl.pallas_call(
        functools.partial(rotate_kernel, tuple(places)),
        in_specs=[WHOLE] * (2 + len(flat)),
        out_specs=[WHOLE] * 3,
        out_shape=[
            jax.ShapeDtypeStruct((cols, rank), F32),
            jax.ShapeDtypeStruct((3 * rank, cols), BF16),
            jax.ShapeDtypeStruct((8, rank), F32),
        ],
        compiler_params=pltpu.CompilerParams(vmem_limit_bytes=24 * MIB),
        cost_estimate=cost(6 * cols * rank * rank, cols * rank * 16),
        name="right_rotate",
    )(*inv, *flat)


def momentum_kernel(first, shi_ref, slo_ref, left_ref, terms_ref, *refs):
    out_ref = refs[-1]
    tile = out_ref.shape[0]
    rows = pl.ds(pl.multiple_of((first + pl.program_id(0)) * tile, tile), tile)
    summed = shi_ref[rows, :].astype(F32) + slo_ref[rows, :].astype(F32)
    out_ref[...] = summed - dot(left_ref[rows, :], terms_ref[...])


def momentum_call(part, parts, shi, slo, left, terms, before=None):
    rows, cols = shi.shape
    rank = left.shape[1] // 3
    tile = 256
    count = max(rows // tile // parts, 1)
    first = part * count
    operands = [in_space(shi, pltpu.VMEM), in_space(slo, pltpu.VMEM), left, terms]
    specs = [WHOLE] * 4
    if before is not None:
        operands.append(before)
        specs.append(pl.BlockSpec(memory_space=pl.ANY))
    return pl.pallas_call(
        functools.partial(momentum_kernel, first),
        grid=(count,),
        in_specs=specs,
        out_specs=pl.BlockSpec((tile, cols), lambda i: (first + i, 0)),
        out_shape=jax.ShapeDtypeStruct((rows, cols), F32),
        input_output_aliases={} if before is None else {4: 0},
        compiler_params=params(24),
        cost_estimate=cost(6 * rows * cols * rank // parts, rows * cols * 4 // parts),
        name="momentum_update",
    )(*operands)


def update_kernel(factor, turned_ref, squares_ref, left_ref, terms_ref, update_ref, basis_ref):
    norms = jnp.sqrt(squares_ref[:1, :] + norm_epsilon)
    tile = update_ref.shape[0]
    step = pl.program_id(0)
    rows = pl.ds(pl.multiple_of(step * tile, tile), tile)
    hi, lo = split2(left_ref[rows, :] * (factor / norms))
    scaled = jnp.concatenate([hi, lo, hi], axis=1)
    update_ref[...] = dot(scaled, terms_ref[...]).astype(BF16)
    share = basis_ref.shape[0]
    part = pl.ds(pl.multiple_of(step * share, 8), share)
    basis_ref[...] = turned_ref[part, :] * (1.0 / norms)


def update_call(factor, turned, squares, left, terms):
    cols, rank = turned.shape
    rows = left.shape[0]
    tile = 256
    share = cols // (rows // tile)
    return pl.pallas_call(
        functools.partial(update_kernel, factor / (1.0 - decay_mu)),
        grid=(rows // tile,),
        in_specs=[WHOLE] * 4,
        out_specs=[
            pl.BlockSpec((tile, cols), lambda i: (i, 0)),
            pl.BlockSpec((share, rank), lambda i: (i, 0)),
        ],
        out_shape=[
            jax.ShapeDtypeStruct((rows, cols), BF16),
            jax.ShapeDtypeStruct((cols, rank), F32),
        ],
        compiler_params=params(24),
        cost_estimate=cost(6 * rows * cols * rank, rows * cols * 2),
        name="update_basis",
    )(turned, squares, left, terms)


def swap(x, axis, pairs):
    return lax.ppermute(x, axis, pairs)


def exchanges(wide):
    core, y, za, zb = 1, 2, 4, 12
    steps = ((core, core), (y, za), (za, y), (zb, zb))
    return [[(i, i ^ bits[i % 2]) for i in range(wide)] for bits in steps]


def add_kernel(a_ref, b_ref, *refs):
    refs[-1][...] = a_ref[...] + b_ref[...]


def add_call(a, b, held):
    return pl.pallas_call(
        add_kernel,
        in_specs=[WHOLE] * (2 + len(held)),
        out_specs=WHOLE,
        out_shape=jax.ShapeDtypeStruct(a.shape, a.dtype),
        compiler_params=pltpu.CompilerParams(vmem_limit_bytes=24 * MIB),
        cost_estimate=cost(a.size, 12 * a.size),
        name="add_pieces",
    )(a, b, *(in_space(x, pltpu.VMEM) for x in held))


def join_kernel(a_ref, b_ref, *refs):
    half = a_ref.shape[0]
    refs[-1][:half, :] = a_ref[...]
    refs[-1][half:, :] = b_ref[...]


def join_call(a, b, held):
    rows, cols = a.shape
    return pl.pallas_call(
        join_kernel,
        in_specs=[WHOLE] * (2 + len(held)),
        out_specs=WHOLE,
        out_shape=jax.ShapeDtypeStruct((2 * rows, cols), a.dtype),
        compiler_params=pltpu.CompilerParams(vmem_limit_bytes=24 * MIB),
        cost_estimate=cost(a.size, 16 * a.size),
        name="join_pieces",
    )(a, b, *(in_space(x, pltpu.VMEM) for x in held))


def wide_sum(steps, keep, send, held):
    core, first, second, third = steps
    got = swap(send, "wide", core)
    for pairs in (first, second):
        h = keep.shape[0] // 2
        total = add_call(keep, got, held)
        send, keep = total[h:], total[:h]
        got = swap(send, "wide", pairs)
    mine = add_call(keep, got, held)
    mine = add_call(mine, swap(mine, "wide", third), held)
    for pairs in (second, first):
        mine = join_call(mine, swap(mine, "wide", pairs), held)
    return mine, swap(mine, "wide", core)


def per_device(narrow, wide, whole_rows, whole_cols, momentum, gradient, right_basis, signs, select):
    rows, cols = momentum.shape
    rank = right_basis.shape[1]
    fast = is_fast(narrow, wide)
    index = lax.axis_index("wide")
    steps = exchanges(wide) if fast else None
    across = [(0, 1), (1, 0)]
    shi, slo, send, keep = left_call(fast, momentum, gradient, right_basis)
    sketch_rows = select.shape[0]
    scale = 1.0 / math.sqrt(sketch_rows)
    if fast:
        share = sketch_rows // wide
        mine = lax.dynamic_slice_in_dim(select, index * share, share)
        first, second = wide_sum(steps, keep, send, (shi, slo))
        left, sketch = sketch_call(fast, first, second, mine, signs, scale, (shi, slo))
        other = swap(sketch, "narrow", across)
        cut = cols * 2 // 7
        (right,) = right_call(left, shi, slo, 0, cut)
        pieces = [[right, swap(right, "narrow", across)]]
        right, sketch = right_call(left, shi, slo, cut, cols, sketch, other)
        pieces.append([right, swap(right, "narrow", across)])
        for pairs in reversed(steps[1:]):
            sketch = jnp.concatenate([sketch, swap(sketch, "wide", pairs)], axis=0)
        sketches = (sketch, swap(sketch, "wide", steps[0]))
    else:
        first, second = lax.psum((keep, send), "wide")
        left, sketch = sketch_call(fast, first, second, select, signs, scale, ())
        sketch = lax.psum(sketch, "narrow")
        sketches = (sketch[: sketch_rows // 2], sketch[sketch_rows // 2 :])
        (right,) = right_call(left, shi, slo, 0, cols)
        pieces = [[lax.psum(right, "narrow")]]
    inv = factor_call(*sketches)
    left_terms, basis = basis_call(inv, left)
    left_terms, pieces[-1][-1] = lax.optimization_barrier((left_terms, pieces[-1][-1]))
    turned, right_terms, squares = rotate_call(inv, pieces)
    if fast:
        momentum_out = None
        for part, pairs in enumerate(steps):
            squares = squares + swap(squares, "wide", pairs)
            momentum_out = momentum_call(
                part, len(steps), shi, slo, left_terms, right_terms, momentum_out
            )
    else:
        squares = lax.psum(squares, "wide")
        momentum_out = momentum_call(0, 1, shi, slo, left_terms, right_terms)
    factor = math.sqrt(whole_rows * whole_cols / rank)
    update, basis_out = update_call(factor, turned, squares, basis, right_terms)
    return momentum_out, basis_out, update


def solution(mesh):
    in_specs = (P("narrow", "wide"), P("narrow", "wide"), P("wide", None), P(), P())
    out_specs = (P("narrow", "wide"), P("wide", None), P("narrow", "wide"))
    narrow, wide = mesh.shape["narrow"], mesh.shape["wide"]

    def whole(momentum, *rest):
        body = functools.partial(per_device, narrow, wide, *momentum.shape)
        return jax.shard_map(
            body, mesh=mesh, in_specs=in_specs, out_specs=out_specs, check_vma=False
        )(momentum, *rest)

    return whole
```

```python
import functools
import math

import jax
import jax.numpy as jnp
from jax import lax
from jax.experimental import pallas as pl
from jax.experimental.pallas import tpu as pltpu
from jax.sharding import PartitionSpec as P

decay_mu = 0.95
norm_epsilon = 1e-06

F32 = jnp.float32
BF16 = jnp.bfloat16
HIGH = lax.Precision.HIGHEST
MIB = 1024 * 1024
WHOLE = pl.BlockSpec(memory_space=pltpu.VMEM)


def split2(x):
    hi = x.astype(BF16)
    return hi, (x - hi.astype(F32)).astype(BF16)


def dot(a, b):
    return jnp.dot(a, b, preferred_element_type=F32)


in_space = pltpu.with_memory_space_constraint


def params(mib):
    return pltpu.CompilerParams(
        vmem_limit_bytes=mib * MIB, dimension_semantics=("arbitrary",)
    )


def cost(flops, bytes_accessed):
    return pl.CostEstimate(
        flops=int(flops), bytes_accessed=int(bytes_accessed), transcendentals=0
    )


TILE = 512
SLOTS = 2


def is_fast(narrow, wide):
    return narrow == 2 and wide == 16


def labels_of(fast):
    if not fast:
        return 0, 4
    index = lax.axis_index("wide")
    core, y, z = index & 1, (index >> 1) & 1, index >> 2
    za = (z >> 1) ^ (z & 1)
    even, odd = 2 * y + za, 4 + 2 * za + y
    return even + core * (odd - even), odd + core * (even - odd)


def left_kernel(
    fast,
    m_hbm,
    g_hbm,
    b_hbm,
    shi_ref,
    slo_ref,
    send_ref,
    keep_ref,
    m_ref,
    g_ref,
    b_ref,
    bhi,
    blo,
    lt,
    sems,
    b_sem,
):
    rows, cols = m_hbm.shape
    rank = b_ref.shape[1]
    block = rank // 8
    tiles = rows // TILE
    labels = labels_of(fast)

    def copies(t):
        source, slot = pl.ds(t * TILE, TILE), pl.ds(t % SLOTS * TILE, TILE)
        return (
            pltpu.make_async_copy(m_hbm.at[source], m_ref.at[slot], sems.at[0, t % SLOTS]),
            pltpu.make_async_copy(g_hbm.at[source], g_ref.at[slot], sems.at[1, t % SLOTS]),
        )

    b_copy = pltpu.make_async_copy(b_hbm, b_ref, b_sem)
    b_copy.start()
    for t in range(min(SLOTS - 1, tiles)):
        for copy in copies(t):
            copy.start()
    b_copy.wait()
    bhi[...], blo[...] = split2(b_ref[...])

    for t in range(tiles):
        for copy in copies(t):
            copy.wait()
        if t + SLOTS - 1 < tiles:
            for copy in copies(t + SLOTS - 1):
                copy.start()
        part, slot = slice(t * TILE, t * TILE + TILE), t % SLOTS * TILE
        slot = slice(slot, slot + TILE)
        hi, lo = split2(m_ref[slot, :] + g_ref[slot, :].astype(F32))
        shi_ref[part, :] = hi
        slo_ref[part, :] = lo
        left = dot(hi, bhi[...]) + (dot(lo, bhi[...]) + dot(hi, blo[...]))
        lt[...] = left.T
        for side, ref in enumerate((keep_ref, send_ref)):
            for q in range(4):
                start = pl.multiple_of(block * (labels[side] ^ q), block)
                ref[block * q : block * q + block, part] = lt[pl.ds(start, block), :]


def left_call(fast, momentum, gradient, right_basis):
    rows, cols = momentum.shape
    rank = right_basis.shape[1]
    part = jax.ShapeDtypeStruct((rank // 2, rows), F32)
    hbm = pl.BlockSpec(memory_space=pltpu.HBM)
    return pl.pallas_call(
        functools.partial(left_kernel, fast),
        in_specs=[hbm] * 3,
        out_specs=[WHOLE] * 4,
        out_shape=[
            pltpu.VMEM((rows, cols), BF16),
            pltpu.VMEM((rows, cols), BF16),
            part,
            part,
        ],
        scratch_shapes=[
            pltpu.VMEM((SLOTS * TILE, cols), F32),
            pltpu.VMEM((SLOTS * TILE, cols), BF16),
            pltpu.VMEM((cols, rank), F32),
            pltpu.VMEM((cols, rank), BF16),
            pltpu.VMEM((cols, rank), BF16),
            pltpu.VMEM((rank, TILE), F32),
            pltpu.SemaphoreType.DMA((2, SLOTS)),
            pltpu.SemaphoreType.DMA,
        ],
        compiler_params=pltpu.CompilerParams(vmem_limit_bytes=24 * MIB),
        cost_estimate=cost(6 * rows * cols * rank, rows * cols * 6),
        name="left_factor",
    )(*(in_space(x, pltpu.HBM) for x in (momentum, gradient, right_basis)))


def entries_kernel(fast, select_ref, signs_ref, *refs):
    entries_ref, column_ref = refs[-2:]
    share, rows = entries_ref.shape
    column_ref[...] = jnp.broadcast_to(
        select_ref[...].astype(F32), (column_ref.shape[1], select_ref.shape[1])
    ).T
    start = pl.multiple_of(lax.axis_index("wide") * share, 8) if fast else 0
    select = column_ref[pl.ds(start, share), :1].astype(jnp.int32)
    first = pl.multiple_of(lax.axis_index("narrow") * rows, rows)
    column = first + lax.broadcasted_iota(jnp.int32, (1, rows), 1)
    bits = jnp.bitwise_and(select, column)
    for shift in (8, 4, 2, 1):
        bits = jnp.bitwise_xor(bits, jnp.right_shift(bits, shift))
    entries = (1 - 2 * jnp.bitwise_and(bits, 1)) * signs_ref[:, pl.ds(first, rows)]
    entries_ref[...] = entries.astype(F32).astype(BF16)


def entries_call(fast, select, share, signs, rows, after, held):
    return pl.pallas_call(
        functools.partial(entries_kernel, fast),
        in_specs=[WHOLE] * 2
        + [pl.BlockSpec(memory_space=pl.ANY)] * len(after)
        + [WHOLE] * len(held),
        out_specs=WHOLE,
        out_shape=jax.ShapeDtypeStruct((share, rows), BF16),
        scratch_shapes=[pltpu.VMEM((select.shape[0], 128), F32)],
        compiler_params=pltpu.CompilerParams(vmem_limit_bytes=24 * MIB),
        cost_estimate=cost(20 * share * rows, 2 * share * rows),
        name="hadamard_signs",
    )(
        select[None, :],
        signs[None, :],
        *after,
        *(in_space(x, pltpu.VMEM) for x in held),
    )


def sketch_kernel(fast, scale, a_ref, b_ref, entries_ref, *refs):
    left_ref, sketch_ref = refs[-2:]
    half, rows = a_ref.shape
    rank = 2 * half
    block = rank // 8
    labels = labels_of(fast)
    for side, ref in enumerate((a_ref, b_ref)):
        for q in range(4):
            start = pl.multiple_of(block * (labels[side] ^ q), block)
            hi, lo = split2(ref[block * q : block * q + block, :])
            left_ref[pl.ds(start, block), :] = hi
            left_ref[pl.ds(pl.multiple_of(rank + start, block), block), :] = lo
    both = lax.dot_general(
        entries_ref[...],
        left_ref[...],
        (((1,), (1,)), ((), ())),
        preferred_element_type=F32,
    )
    sketch_ref[...] = (both[:, :rank] + both[:, rank:]) * scale


def sketch_call(fast, first, second, entries, scale, held):
    half, rows = first.shape
    rank = 2 * half
    share = entries.shape[0]
    return pl.pallas_call(
        functools.partial(sketch_kernel, fast, scale),
        in_specs=[WHOLE] * (3 + len(held)),
        out_specs=[WHOLE] * 2,
        out_shape=[
            jax.ShapeDtypeStruct((2 * rank, rows), BF16),
            jax.ShapeDtypeStruct((share, rank), F32),
        ],
        compiler_params=pltpu.CompilerParams(vmem_limit_bytes=24 * MIB),
        cost_estimate=cost(4 * share * rank * rows, rows * rank * 8),
        name="sketch_rows",
    )(first, second, entries, *(in_space(x, pltpu.VMEM) for x in held))


def right_kernel(first, left_ref, shi_ref, slo_ref, *refs):
    if len(refs) > 1:
        mine_ref, other_ref, w_ref, sketch_ref = refs
        sketch_ref[...] = mine_ref[...] + other_ref[...]
    else:
        (w_ref,) = refs
    rank, cols = w_ref.shape
    for start in range(0, cols, 256):
        stop = min(start + 256, cols)
        source = slice(first + start, first + stop)
        both = dot(left_ref[...], shi_ref[:, source])
        last = dot(left_ref[:rank, :], slo_ref[:, source])
        w_ref[:, start:stop] = (both[:rank] + both[rank:]) + last


def right_call(left, shi, slo, first, stop, *sketches):
    rows = shi.shape[0]
    rank = left.shape[0] // 2
    cols = stop - first
    outs = [jax.ShapeDtypeStruct((rank, cols), F32)]
    if sketches:
        outs.append(jax.ShapeDtypeStruct(sketches[0].shape, F32))
    return pl.pallas_call(
        functools.partial(right_kernel, first),
        in_specs=[WHOLE] * (3 + len(sketches)),
        out_specs=[WHOLE] * len(outs),
        out_shape=outs,
        compiler_params=pltpu.CompilerParams(vmem_limit_bytes=24 * MIB),
        cost_estimate=cost(6 * rows * cols * rank, rows * cols * 4),
        name="right_factor",
    )(left, in_space(shi, pltpu.VMEM), in_space(slo, pltpu.VMEM), *sketches)


def eliminate(block):
    n = block.shape[0]
    groups = [block[8 * g : 8 * g + 8, :] for g in range(n // 8)]
    lane = lax.broadcasted_iota(jnp.int32, (8, n), 1)
    out = []
    for k in range(0, n, 4):
        g0, o = k // 8, k % 8
        rows = [groups[g0][o + j : o + j + 1, :] for j in range(4)]

        def entry(i, j):
            return jnp.broadcast_to(rows[i][:, k + j : k + j + 1], (8, n))

        u = [[entry(i, j) if j >= i else None for j in range(4)] for i in range(4)]
        inv = []
        low = [[None] * 4 for _ in range(4)]
        for i in range(4):
            inv.append(1.0 / u[i][i])
            for r in range(i + 1, 4):
                low[r][i] = u[i][r] * inv[i]
                for j in range(r, 4):
                    u[r][j] = u[r][j] - low[r][i] * u[i][j]
        inside = jnp.logical_and(lane >= k, lane < k + 4)
        q = []
        for i in range(4):
            base = jnp.where(inside, 0.0, jnp.broadcast_to(rows[i], (8, n)))
            base = jnp.where(lane == k + i, 1.0, base)
            for j in range(i):
                base = base - low[i][j] * q[j]
            q.append(base)
            out.append(jnp.where(lane <= k + i, base * lax.rsqrt(u[i][i]), 0.0)[:1])
        for g in range(g0 if o == 0 else g0 + 1, n // 8):
            x = groups[g]
            new = jnp.where(inside, 0.0, x)
            h = []
            for i in range(4):
                c = jnp.broadcast_to(x[:, k + i : k + i + 1], (8, n))
                for j in range(i):
                    c = c - h[j] * u[j][i]
                h.append(c * inv[i])
                new = new - h[i] * q[i]
            groups[g] = new
    return jnp.concatenate(out, axis=0)


def dot_high(a, b, dims=((1,), (0,))):
    return lax.dot_general(
        a, b, (dims, ((), ())), precision=HIGH, preferred_element_type=F32
    )


def factor_kernel(a_ref, b_ref, hi_ref, lo_ref):
    sketch = jnp.concatenate([a_ref[...], b_ref[...]], axis=0)
    gram = dot_high(sketch, sketch, ((0,), (0,)))
    half = gram.shape[0] // 2
    inv11 = eliminate(gram[:half, :half])
    l21 = dot_high(gram[half:, :half], inv11, ((1,), (1,)))
    inv22 = eliminate(gram[half:, half:] - dot_high(l21, l21, ((1,), (1,))))
    inv21 = -dot_high(inv22, dot_high(l21, inv11))
    top = jnp.concatenate([inv11, jnp.zeros_like(inv11)], axis=1)
    inverse = jnp.concatenate([top, jnp.concatenate([inv21, inv22], axis=1)], axis=0)
    hi_ref[...], lo_ref[...] = split2(inverse)


def factor_call(first, second):
    rank = first.shape[1]
    out = jax.ShapeDtypeStruct((rank, rank), BF16)
    return pl.pallas_call(
        factor_kernel,
        in_specs=[WHOLE] * 2,
        out_specs=[WHOLE] * 2,
        out_shape=[out, out],
        compiler_params=pltpu.CompilerParams(vmem_limit_bytes=24 * MIB),
        cost_estimate=cost(1e6, 1e5),
        name="factor_inverse",
    )(first, second)


def basis_kernel(hi_ref, lo_ref, raw_ref, terms_ref, basis_ref):
    rank = hi_ref.shape[0]
    hi, lo = raw_ref[:rank, :], raw_ref[rank:, :]
    basis = dot(hi_ref[...], hi) + (dot(hi_ref[...], lo) + dot(lo_ref[...], hi))
    basis = basis.T
    basis_ref[...] = basis
    hi, lo = split2(basis)
    terms_ref[...] = jnp.concatenate([hi, lo, hi], axis=1)


def basis_call(inv, raw):
    rows = raw.shape[1]
    rank = inv[0].shape[0]
    tile = 256
    inv_spec = pl.BlockSpec((rank, rank), lambda i: (0, 0))
    return pl.pallas_call(
        basis_kernel,
        grid=(rows // tile,),
        in_specs=[inv_spec] * 2 + [pl.BlockSpec((2 * rank, tile), lambda i: (0, i))],
        out_specs=[
            pl.BlockSpec((tile, 3 * rank), lambda i: (i, 0)),
            pl.BlockSpec((tile, rank), lambda i: (i, 0)),
        ],
        out_shape=[
            jax.ShapeDtypeStruct((rows, 3 * rank), BF16),
            jax.ShapeDtypeStruct((rows, rank), F32),
        ],
        compiler_params=params(24),
        cost_estimate=cost(1e6, 1e5),
        name="left_basis",
    )(*inv, raw)


def rotate_kernel(pieces, hi_ref, lo_ref, *refs):
    parts, (turned_ref, terms_ref, squares_ref) = refs[:-3], refs[-3:]
    rank = hi_ref.shape[0]
    squares = jnp.zeros((rank, 1), F32)
    start = 0
    for piece in pieces:
        total = piece[0]
        total = parts[total][...]
        for other in piece[1:]:
            total = total + parts[other][...]
        stop = start + total.shape[1]
        hi, lo = split2(total)
        right = dot(hi_ref[...], hi) + (dot(hi_ref[...], lo) + dot(lo_ref[...], hi))
        turned_ref[start:stop, :] = right.T
        hi, lo = split2((1.0 - decay_mu) * right)
        terms_ref[:rank, start:stop] = hi
        terms_ref[rank : 2 * rank, start:stop] = hi
        terms_ref[2 * rank :, start:stop] = lo
        squares = squares + jnp.sum(right * right, axis=1, keepdims=True)
        start = stop
    squares_ref[...] = jnp.broadcast_to(squares, (rank, 128)).T[:8, :]


def rotate_call(inv, pieces):
    rank = inv[0].shape[0]
    cols = sum(piece[0].shape[1] for piece in pieces)
    flat, places = [], []
    for piece in pieces:
        places.append(tuple(range(len(flat), len(flat) + len(piece))))
        flat.extend(piece)
    return pl.pallas_call(
        functools.partial(rotate_kernel, tuple(places)),
        in_specs=[WHOLE] * (2 + len(flat)),
        out_specs=[WHOLE] * 3,
        out_shape=[
            jax.ShapeDtypeStruct((cols, rank), F32),
            jax.ShapeDtypeStruct((3 * rank, cols), BF16),
            jax.ShapeDtypeStruct((8, rank), F32),
        ],
        compiler_params=pltpu.CompilerParams(vmem_limit_bytes=24 * MIB),
        cost_estimate=cost(6 * cols * rank * rank, cols * rank * 16),
        name="right_rotate",
    )(*inv, *flat)


def momentum_kernel(first, shi_ref, slo_ref, left_ref, terms_ref, *refs):
    out_ref = refs[-1]
    tile = out_ref.shape[0]
    rows = pl.ds(pl.multiple_of((first + pl.program_id(0)) * tile, tile), tile)
    summed = shi_ref[rows, :].astype(F32) + slo_ref[rows, :].astype(F32)
    out_ref[...] = summed - dot(left_ref[rows, :], terms_ref[...])


def momentum_call(part, parts, shi, slo, left, terms, before=None):
    rows, cols = shi.shape
    rank = left.shape[1] // 3
    tile = 256
    count = max(rows // tile // parts, 1)
    first = part * count
    operands = [in_space(shi, pltpu.VMEM), in_space(slo, pltpu.VMEM), left, terms]
    specs = [WHOLE] * 4
    if before is not None:
        operands.append(before)
        specs.append(pl.BlockSpec(memory_space=pl.ANY))
    return pl.pallas_call(
        functools.partial(momentum_kernel, first),
        grid=(count,),
        in_specs=specs,
        out_specs=pl.BlockSpec((tile, cols), lambda i: (first + i, 0)),
        out_shape=jax.ShapeDtypeStruct((rows, cols), F32),
        input_output_aliases={} if before is None else {4: 0},
        compiler_params=params(24),
        cost_estimate=cost(6 * rows * cols * rank // parts, rows * cols * 4 // parts),
        name="momentum_update",
    )(*operands)


def update_kernel(factor, turned_ref, squares_ref, left_ref, terms_ref, update_ref, basis_ref):
    norms = jnp.sqrt(squares_ref[:1, :] + norm_epsilon)
    tile = update_ref.shape[0]
    step = pl.program_id(0)
    rows = pl.ds(pl.multiple_of(step * tile, tile), tile)
    hi, lo = split2(left_ref[rows, :] * (factor / norms))
    scaled = jnp.concatenate([hi, lo, hi], axis=1)
    update_ref[...] = dot(scaled, terms_ref[...]).astype(BF16)
    share = basis_ref.shape[0]
    part = pl.ds(pl.multiple_of(step * share, 8), share)
    basis_ref[...] = turned_ref[part, :] * (1.0 / norms)


def update_call(factor, turned, squares, left, terms):
    cols, rank = turned.shape
    rows = left.shape[0]
    tile = 256
    share = cols // (rows // tile)
    return pl.pallas_call(
        functools.partial(update_kernel, factor / (1.0 - decay_mu)),
        grid=(rows // tile,),
        in_specs=[WHOLE] * 4,
        out_specs=[
            pl.BlockSpec((tile, cols), lambda i: (i, 0)),
            pl.BlockSpec((share, rank), lambda i: (i, 0)),
        ],
        out_shape=[
            jax.ShapeDtypeStruct((rows, cols), BF16),
            jax.ShapeDtypeStruct((cols, rank), F32),
        ],
        compiler_params=params(24),
        cost_estimate=cost(6 * rows * cols * rank, rows * cols * 2),
        name="update_basis",
    )(turned, squares, left, terms)


def swap(x, axis, pairs):
    return lax.ppermute(x, axis, pairs)


def exchanges(wide):
    core, y, za, zb = 1, 2, 4, 12
    steps = ((core, core), (y, za), (za, y), (zb, zb))
    return [[(i, i ^ bits[i % 2]) for i in range(wide)] for bits in steps]


def add_kernel(a_ref, b_ref, *refs):
    refs[-1][...] = a_ref[...] + b_ref[...]


def add_call(a, b, held):
    return pl.pallas_call(
        add_kernel,
        in_specs=[WHOLE] * (2 + len(held)),
        out_specs=WHOLE,
        out_shape=jax.ShapeDtypeStruct(a.shape, a.dtype),
        compiler_params=pltpu.CompilerParams(vmem_limit_bytes=24 * MIB),
        cost_estimate=cost(a.size, 12 * a.size),
        name="add_pieces",
    )(a, b, *(in_space(x, pltpu.VMEM) for x in held))


def join_kernel(a_ref, b_ref, *refs):
    half = a_ref.shape[0]
    refs[-1][:half, :] = a_ref[...]
    refs[-1][half:, :] = b_ref[...]


def join_call(a, b, held):
    rows, cols = a.shape
    return pl.pallas_call(
        join_kernel,
        in_specs=[WHOLE] * (2 + len(held)),
        out_specs=WHOLE,
        out_shape=jax.ShapeDtypeStruct((2 * rows, cols), a.dtype),
        compiler_params=pltpu.CompilerParams(vmem_limit_bytes=24 * MIB),
        cost_estimate=cost(a.size, 16 * a.size),
        name="join_pieces",
    )(a, b, *(in_space(x, pltpu.VMEM) for x in held))


def wide_sum(steps, keep, send, held):
    core, first, second, third = steps
    got = swap(send, "wide", core)
    for pairs in (first, second):
        h = keep.shape[0] // 2
        total = add_call(keep, got, held)
        send, keep = total[h:], total[:h]
        got = swap(send, "wide", pairs)
    mine = add_call(keep, got, held)
    mine = add_call(mine, swap(mine, "wide", third), held)
    for pairs in (second, first):
        mine = join_call(mine, swap(mine, "wide", pairs), held)
    return mine, swap(mine, "wide", core)


def per_device(narrow, wide, whole_rows, whole_cols, momentum, gradient, right_basis, signs, select):
    rows, cols = momentum.shape
    rank = right_basis.shape[1]
    fast = is_fast(narrow, wide)
    steps = exchanges(wide) if fast else None
    across = [(0, 1), (1, 0)]
    shi, slo, send, keep = left_call(fast, momentum, gradient, right_basis)
    sketch_rows = select.shape[0]
    scale = 1.0 / math.sqrt(sketch_rows)
    if fast:
        share = sketch_rows // wide
        first, second = wide_sum(steps, keep, send, (shi, slo))
        entries = entries_call(fast, select, share, signs, rows, (first,), (shi, slo))
        left, sketch = sketch_call(fast, first, second, entries, scale, (shi, slo))
        other = swap(sketch, "narrow", across)
        cut = cols // 256 * 128
        (right,) = right_call(left, shi, slo, 0, cut)
        pieces = [[right, swap(right, "narrow", across)]]
        right, sketch = right_call(left, shi, slo, cut, cols, sketch, other)
        pieces.append([right, swap(right, "narrow", across)])
        for pairs in reversed(steps[1:]):
            sketch = join_call(sketch, swap(sketch, "wide", pairs), ())
        sketches = (sketch, swap(sketch, "wide", steps[0]))
    else:
        first, second = lax.psum((keep, send), "wide")
        entries = entries_call(fast, select, sketch_rows, signs, rows, (), ())
        left, sketch = sketch_call(fast, first, second, entries, scale, ())
        sketch = lax.psum(sketch, "narrow")
        sketches = (sketch[: sketch_rows // 2], sketch[sketch_rows // 2 :])
        (right,) = right_call(left, shi, slo, 0, cols)
        pieces = [[lax.psum(right, "narrow")]]
    inv = factor_call(*sketches)
    left_terms, basis = basis_call(inv, left)
    left_terms, pieces[-1][-1] = lax.optimization_barrier((left_terms, pieces[-1][-1]))
    turned, right_terms, squares = rotate_call(inv, pieces)
    if fast:
        momentum_out = None
        for part, pairs in enumerate(steps):
            squares = add_call(squares, swap(squares, "wide", pairs), ())
            momentum_out = momentum_call(
                part, len(steps), shi, slo, left_terms, right_terms, momentum_out
            )
    else:
        squares = lax.psum(squares, "wide")
        momentum_out = momentum_call(0, 1, shi, slo, left_terms, right_terms)
    factor = math.sqrt(whole_rows * whole_cols / rank)
    update, basis_out = update_call(factor, turned, squares, basis, right_terms)
    return momentum_out, basis_out, update


def solution(mesh):
    in_specs = (P("narrow", "wide"), P("narrow", "wide"), P("wide", None), P(), P())
    out_specs = (P("narrow", "wide"), P("wide", None), P("narrow", "wide"))
    narrow, wide = mesh.shape["narrow"], mesh.shape["wide"]

    def whole(momentum, *rest):
        body = functools.partial(per_device, narrow, wide, *momentum.shape)
        return jax.shard_map(
            body, mesh=mesh, in_specs=in_specs, out_specs=out_specs, check_vma=False
        )(momentum, *rest)

    return whole
```

```python
import functools
import math

import jax
import jax.numpy as jnp
from jax import lax
from jax.experimental import pallas as pl
from jax.experimental.pallas import tpu as pltpu
from jax.sharding import PartitionSpec as P

decay_mu = 0.95
norm_epsilon = 1e-06

F32 = jnp.float32
BF16 = jnp.bfloat16
HIGH = lax.Precision.HIGHEST
MIB = 1024 * 1024
WHOLE = pl.BlockSpec(memory_space=pltpu.VMEM)


def split2(x):
    hi = x.astype(BF16)
    return hi, (x - hi.astype(F32)).astype(BF16)


def dot(a, b):
    return jnp.dot(a, b, preferred_element_type=F32)


in_space = pltpu.with_memory_space_constraint


def params(mib):
    return pltpu.CompilerParams(
        vmem_limit_bytes=mib * MIB, dimension_semantics=("arbitrary",)
    )


def cost(flops, bytes_accessed):
    return pl.CostEstimate(
        flops=int(flops), bytes_accessed=int(bytes_accessed), transcendentals=0
    )


TILE = 512
SLOTS = 2


def is_fast(narrow, wide):
    return narrow == 2 and wide == 16


def labels_of(fast):
    if not fast:
        return 0, 4
    index = lax.axis_index("wide")
    core, y, z = index & 1, (index >> 1) & 1, index >> 2
    za = (z >> 1) ^ (z & 1)
    even, odd = 2 * y + za, 4 + 2 * za + y
    return even + core * (odd - even), odd + core * (even - odd)


def left_kernel(
    fast,
    m_hbm,
    g_hbm,
    b_hbm,
    shi_ref,
    slo_ref,
    send_ref,
    keep_ref,
    m_ref,
    g_ref,
    b_ref,
    bhi,
    blo,
    lt,
    sems,
    b_sem,
):
    rows, cols = m_hbm.shape
    rank = b_ref.shape[1]
    block = rank // 8
    tiles = rows // TILE
    labels = labels_of(fast)

    def copies(t):
        source, slot = pl.ds(t * TILE, TILE), pl.ds(t % SLOTS * TILE, TILE)
        return (
            pltpu.make_async_copy(m_hbm.at[source], m_ref.at[slot], sems.at[0, t % SLOTS]),
            pltpu.make_async_copy(g_hbm.at[source], g_ref.at[slot], sems.at[1, t % SLOTS]),
        )

    b_copy = pltpu.make_async_copy(b_hbm, b_ref, b_sem)
    b_copy.start()
    for t in range(min(SLOTS - 1, tiles)):
        for copy in copies(t):
            copy.start()
    b_copy.wait()
    bhi[...], blo[...] = split2(b_ref[...])

    for t in range(tiles):
        for copy in copies(t):
            copy.wait()
        if t + SLOTS - 1 < tiles:
            for copy in copies(t + SLOTS - 1):
                copy.start()
        part, slot = slice(t * TILE, t * TILE + TILE), t % SLOTS * TILE
        slot = slice(slot, slot + TILE)
        hi, lo = split2(m_ref[slot, :] + g_ref[slot, :].astype(F32))
        shi_ref[part, :] = hi
        slo_ref[part, :] = lo
        both = dot(jnp.concatenate([hi, lo], axis=0), bhi[...])
        left = (both[:TILE] + both[TILE:]) + dot(hi, blo[...])
        lt[...] = left.T
        for side, ref in enumerate((keep_ref, send_ref)):
            for q in range(4):
                start = pl.multiple_of(block * (labels[side] ^ q), block)
                ref[block * q : block * q + block, part] = lt[pl.ds(start, block), :]


def left_call(fast, momentum, gradient, right_basis):
    rows, cols = momentum.shape
    rank = right_basis.shape[1]
    part = jax.ShapeDtypeStruct((rank // 2, rows), F32)
    hbm = pl.BlockSpec(memory_space=pltpu.HBM)
    return pl.pallas_call(
        functools.partial(left_kernel, fast),
        in_specs=[hbm] * 3,
        out_specs=[WHOLE] * 4,
        out_shape=[
            pltpu.VMEM((rows, cols), BF16),
            pltpu.VMEM((rows, cols), BF16),
            part,
            part,
        ],
        scratch_shapes=[
            pltpu.VMEM((SLOTS * TILE, cols), F32),
            pltpu.VMEM((SLOTS * TILE, cols), BF16),
            pltpu.VMEM((cols, rank), F32),
            pltpu.VMEM((cols, rank), BF16),
            pltpu.VMEM((cols, rank), BF16),
            pltpu.VMEM((rank, TILE), F32),
            pltpu.SemaphoreType.DMA((2, SLOTS)),
            pltpu.SemaphoreType.DMA,
        ],
        compiler_params=pltpu.CompilerParams(vmem_limit_bytes=24 * MIB),
        cost_estimate=cost(6 * rows * cols * rank, rows * cols * 6),
        name="left_factor",
    )(*(in_space(x, pltpu.HBM) for x in (momentum, gradient, right_basis)))


def entries_kernel(fast, select_ref, signs_ref, *refs):
    entries_ref, column_ref = refs[-2:]
    share, rows = entries_ref.shape
    column_ref[...] = jnp.broadcast_to(
        select_ref[...].astype(F32), (column_ref.shape[1], select_ref.shape[1])
    ).T
    start = pl.multiple_of(lax.axis_index("wide") * share, 8) if fast else 0
    select = column_ref[pl.ds(start, share), :1].astype(jnp.int32)
    first = pl.multiple_of(lax.axis_index("narrow") * rows, rows)
    column = first + lax.broadcasted_iota(jnp.int32, (1, rows), 1)
    bits = jnp.bitwise_and(select, column)
    for shift in (8, 4, 2, 1):
        bits = jnp.bitwise_xor(bits, jnp.right_shift(bits, shift))
    entries = (1 - 2 * jnp.bitwise_and(bits, 1)) * signs_ref[:, pl.ds(first, rows)]
    entries_ref[...] = entries.astype(F32).astype(BF16)


def entries_call(fast, select, share, signs, rows, after, held):
    return pl.pallas_call(
        functools.partial(entries_kernel, fast),
        in_specs=[WHOLE] * 2
        + [pl.BlockSpec(memory_space=pl.ANY)] * len(after)
        + [WHOLE] * len(held),
        out_specs=WHOLE,
        out_shape=jax.ShapeDtypeStruct((share, rows), BF16),
        scratch_shapes=[pltpu.VMEM((select.shape[0], 128), F32)],
        compiler_params=pltpu.CompilerParams(vmem_limit_bytes=24 * MIB),
        cost_estimate=cost(20 * share * rows, 2 * share * rows),
        name="hadamard_signs",
    )(
        select[None, :],
        signs[None, :],
        *after,
        *(in_space(x, pltpu.VMEM) for x in held),
    )


def sketch_kernel(fast, scale, a_ref, b_ref, entries_ref, *refs):
    left_ref, sketch_ref = refs[-2:]
    half, rows = a_ref.shape
    rank = 2 * half
    block = rank // 8
    labels = labels_of(fast)
    for side, ref in enumerate((a_ref, b_ref)):
        for q in range(4):
            start = pl.multiple_of(block * (labels[side] ^ q), block)
            hi, lo = split2(ref[block * q : block * q + block, :])
            left_ref[pl.ds(start, block), :] = hi
            left_ref[pl.ds(pl.multiple_of(rank + start, block), block), :] = lo
    both = lax.dot_general(
        entries_ref[...],
        left_ref[...],
        (((1,), (1,)), ((), ())),
        preferred_element_type=F32,
    )
    sketch_ref[...] = (both[:, :rank] + both[:, rank:]) * scale


def sketch_call(fast, first, second, entries, scale, held):
    half, rows = first.shape
    rank = 2 * half
    share = entries.shape[0]
    return pl.pallas_call(
        functools.partial(sketch_kernel, fast, scale),
        in_specs=[WHOLE] * (3 + len(held)),
        out_specs=[WHOLE] * 2,
        out_shape=[
            jax.ShapeDtypeStruct((2 * rank, rows), BF16),
            jax.ShapeDtypeStruct((share, rank), F32),
        ],
        compiler_params=pltpu.CompilerParams(vmem_limit_bytes=24 * MIB),
        cost_estimate=cost(4 * share * rank * rows, rows * rank * 8),
        name="sketch_rows",
    )(first, second, entries, *(in_space(x, pltpu.VMEM) for x in held))


def right_kernel(first, left_ref, shi_ref, slo_ref, *refs):
    if len(refs) > 1:
        mine_ref, other_ref, w_ref, sketch_ref = refs
        sketch_ref[...] = mine_ref[...] + other_ref[...]
    else:
        (w_ref,) = refs
    rank, cols = w_ref.shape
    for start in range(0, cols, 256):
        stop = min(start + 256, cols)
        source = slice(first + start, first + stop)
        both = dot(left_ref[...], shi_ref[:, source])
        last = dot(left_ref[:rank, :], slo_ref[:, source])
        w_ref[:, start:stop] = (both[:rank] + both[rank:]) + last


def right_call(left, shi, slo, first, stop, *sketches):
    rows = shi.shape[0]
    rank = left.shape[0] // 2
    cols = stop - first
    outs = [jax.ShapeDtypeStruct((rank, cols), F32)]
    if sketches:
        outs.append(jax.ShapeDtypeStruct(sketches[0].shape, F32))
    return pl.pallas_call(
        functools.partial(right_kernel, first),
        in_specs=[WHOLE] * (3 + len(sketches)),
        out_specs=[WHOLE] * len(outs),
        out_shape=outs,
        compiler_params=pltpu.CompilerParams(vmem_limit_bytes=24 * MIB),
        cost_estimate=cost(6 * rows * cols * rank, rows * cols * 4),
        name="right_factor",
    )(left, in_space(shi, pltpu.VMEM), in_space(slo, pltpu.VMEM), *sketches)


def eliminate(block):
    n = block.shape[0]
    groups = [block[8 * g : 8 * g + 8, :] for g in range(n // 8)]
    lane = lax.broadcasted_iota(jnp.int32, (8, n), 1)
    out = []
    for k in range(0, n, 4):
        g0, o = k // 8, k % 8
        rows = [groups[g0][o + j : o + j + 1, :] for j in range(4)]

        def entry(i, j):
            return jnp.broadcast_to(rows[i][:, k + j : k + j + 1], (8, n))

        u = [[entry(i, j) if j >= i else None for j in range(4)] for i in range(4)]
        inv = []
        low = [[None] * 4 for _ in range(4)]
        for i in range(4):
            inv.append(1.0 / u[i][i])
            for r in range(i + 1, 4):
                low[r][i] = u[i][r] * inv[i]
                for j in range(r, 4):
                    u[r][j] = u[r][j] - low[r][i] * u[i][j]
        inside = jnp.logical_and(lane >= k, lane < k + 4)
        q = []
        for i in range(4):
            base = jnp.where(inside, 0.0, jnp.broadcast_to(rows[i], (8, n)))
            base = jnp.where(lane == k + i, 1.0, base)
            for j in range(i):
                base = base - low[i][j] * q[j]
            q.append(base)
            out.append(jnp.where(lane <= k + i, base * lax.rsqrt(u[i][i]), 0.0)[:1])
        for g in range(g0 if o == 0 else g0 + 1, n // 8):
            x = groups[g]
            new = jnp.where(inside, 0.0, x)
            h = []
            for i in range(4):
                c = jnp.broadcast_to(x[:, k + i : k + i + 1], (8, n))
                for j in range(i):
                    c = c - h[j] * u[j][i]
                h.append(c * inv[i])
                new = new - h[i] * q[i]
            groups[g] = new
    return jnp.concatenate(out, axis=0)


def dot_high(a, b, dims=((1,), (0,))):
    return lax.dot_general(
        a, b, (dims, ((), ())), precision=HIGH, preferred_element_type=F32
    )


def factor_kernel(a_ref, b_ref, hi_ref, lo_ref):
    sketch = jnp.concatenate([a_ref[...], b_ref[...]], axis=0)
    gram = dot_high(sketch, sketch, ((0,), (0,)))
    half = gram.shape[0] // 2
    inv11 = eliminate(gram[:half, :half])
    l21 = dot_high(gram[half:, :half], inv11, ((1,), (1,)))
    inv22 = eliminate(gram[half:, half:] - dot_high(l21, l21, ((1,), (1,))))
    inv21 = -dot_high(inv22, dot_high(l21, inv11))
    top = jnp.concatenate([inv11, jnp.zeros_like(inv11)], axis=1)
    inverse = jnp.concatenate([top, jnp.concatenate([inv21, inv22], axis=1)], axis=0)
    hi_ref[...], lo_ref[...] = split2(inverse)


def factor_call(first, second):
    rank = first.shape[1]
    out = jax.ShapeDtypeStruct((rank, rank), BF16)
    return pl.pallas_call(
        factor_kernel,
        in_specs=[WHOLE] * 2,
        out_specs=[WHOLE] * 2,
        out_shape=[out, out],
        compiler_params=pltpu.CompilerParams(vmem_limit_bytes=24 * MIB),
        cost_estimate=cost(1e6, 1e5),
        name="factor_inverse",
    )(first, second)


def basis_kernel(hi_ref, lo_ref, raw_ref, terms_ref, basis_ref):
    rank = hi_ref.shape[0]
    hi, lo = raw_ref[:rank, :], raw_ref[rank:, :]
    basis = dot(hi_ref[...], hi) + (dot(hi_ref[...], lo) + dot(lo_ref[...], hi))
    basis = basis.T
    basis_ref[...] = basis
    hi, lo = split2(basis)
    terms_ref[...] = jnp.concatenate([hi, lo, hi], axis=1)


def basis_call(inv, raw):
    rows = raw.shape[1]
    rank = inv[0].shape[0]
    tile = 256
    inv_spec = pl.BlockSpec((rank, rank), lambda i: (0, 0))
    return pl.pallas_call(
        basis_kernel,
        grid=(rows // tile,),
        in_specs=[inv_spec] * 2 + [pl.BlockSpec((2 * rank, tile), lambda i: (0, i))],
        out_specs=[
            pl.BlockSpec((tile, 3 * rank), lambda i: (i, 0)),
            pl.BlockSpec((tile, rank), lambda i: (i, 0)),
        ],
        out_shape=[
            jax.ShapeDtypeStruct((rows, 3 * rank), BF16),
            jax.ShapeDtypeStruct((rows, rank), F32),
        ],
        compiler_params=params(24),
        cost_estimate=cost(1e6, 1e5),
        name="left_basis",
    )(*inv, raw)


def rotate_kernel(pieces, hi_ref, lo_ref, *refs):
    parts, (turned_ref, terms_ref, squares_ref) = refs[:-3], refs[-3:]
    rank = hi_ref.shape[0]
    squares = jnp.zeros((rank, 1), F32)
    start = 0
    for piece in pieces:
        total = piece[0]
        total = parts[total][...]
        for other in piece[1:]:
            total = total + parts[other][...]
        stop = start + total.shape[1]
        hi, lo = split2(total)
        right = dot(hi_ref[...], hi) + (dot(hi_ref[...], lo) + dot(lo_ref[...], hi))
        turned_ref[start:stop, :] = right.T
        hi, lo = split2((1.0 - decay_mu) * right)
        terms_ref[:rank, start:stop] = hi
        terms_ref[rank : 2 * rank, start:stop] = hi
        terms_ref[2 * rank :, start:stop] = lo
        squares = squares + jnp.sum(right * right, axis=1, keepdims=True)
        start = stop
    squares_ref[...] = jnp.broadcast_to(squares, (rank, 128)).T[:8, :]


def rotate_call(inv, pieces):
    rank = inv[0].shape[0]
    cols = sum(piece[0].shape[1] for piece in pieces)
    flat, places = [], []
    for piece in pieces:
        places.append(tuple(range(len(flat), len(flat) + len(piece))))
        flat.extend(piece)
    return pl.pallas_call(
        functools.partial(rotate_kernel, tuple(places)),
        in_specs=[WHOLE] * (2 + len(flat)),
        out_specs=[WHOLE] * 3,
        out_shape=[
            jax.ShapeDtypeStruct((cols, rank), F32),
            jax.ShapeDtypeStruct((3 * rank, cols), BF16),
            jax.ShapeDtypeStruct((8, rank), F32),
        ],
        compiler_params=pltpu.CompilerParams(vmem_limit_bytes=24 * MIB),
        cost_estimate=cost(6 * cols * rank * rank, cols * rank * 16),
        name="right_rotate",
    )(*inv, *flat)


def momentum_kernel(first, shi_ref, slo_ref, left_ref, terms_ref, *refs):
    out_ref = refs[-1]
    tile = out_ref.shape[0]
    rows = pl.ds(pl.multiple_of((first + pl.program_id(0)) * tile, tile), tile)
    summed = shi_ref[rows, :].astype(F32) + slo_ref[rows, :].astype(F32)
    out_ref[...] = summed - dot(left_ref[rows, :], terms_ref[...])


def momentum_call(part, parts, shi, slo, left, terms, before=None):
    rows, cols = shi.shape
    rank = left.shape[1] // 3
    tile = 256
    count = max(rows // tile // parts, 1)
    first = part * count
    operands = [in_space(shi, pltpu.VMEM), in_space(slo, pltpu.VMEM), left, terms]
    specs = [WHOLE] * 4
    if before is not None:
        operands.append(before)
        specs.append(pl.BlockSpec(memory_space=pl.ANY))
    return pl.pallas_call(
        functools.partial(momentum_kernel, first),
        grid=(count,),
        in_specs=specs,
        out_specs=pl.BlockSpec((tile, cols), lambda i: (first + i, 0)),
        out_shape=jax.ShapeDtypeStruct((rows, cols), F32),
        input_output_aliases={} if before is None else {4: 0},
        compiler_params=params(24),
        cost_estimate=cost(6 * rows * cols * rank // parts, rows * cols * 4 // parts),
        name="momentum_update",
    )(*operands)


def update_kernel(factor, turned_ref, squares_ref, left_ref, terms_ref, update_ref, basis_ref):
    norms = jnp.sqrt(squares_ref[:1, :] + norm_epsilon)
    tile = update_ref.shape[0]
    step = pl.program_id(0)
    rows = pl.ds(pl.multiple_of(step * tile, tile), tile)
    hi, lo = split2(left_ref[rows, :] * (factor / norms))
    scaled = jnp.concatenate([hi, lo, hi], axis=1)
    update_ref[...] = dot(scaled, terms_ref[...]).astype(BF16)
    share = basis_ref.shape[0]
    part = pl.ds(pl.multiple_of(step * share, 8), share)
    basis_ref[...] = turned_ref[part, :] * (1.0 / norms)


def update_call(factor, turned, squares, left, terms):
    cols, rank = turned.shape
    rows = left.shape[0]
    tile = min(rows, 512)
    share = cols // (rows // tile)
    return pl.pallas_call(
        functools.partial(update_kernel, factor / (1.0 - decay_mu)),
        grid=(rows // tile,),
        in_specs=[WHOLE] * 4,
        out_specs=[
            pl.BlockSpec((tile, cols), lambda i: (i, 0)),
            pl.BlockSpec((share, rank), lambda i: (i, 0)),
        ],
        out_shape=[
            jax.ShapeDtypeStruct((rows, cols), BF16),
            jax.ShapeDtypeStruct((cols, rank), F32),
        ],
        compiler_params=params(24),
        cost_estimate=cost(6 * rows * cols * rank, rows * cols * 2),
        name="update_basis",
    )(turned, squares, left, terms)


def swap(x, axis, pairs):
    return lax.ppermute(x, axis, pairs)


def exchanges(wide):
    core, y, za, zb = 1, 2, 4, 12
    steps = ((core, core), (y, za), (za, y), (zb, zb))
    return [[(i, i ^ bits[i % 2]) for i in range(wide)] for bits in steps]


def add_kernel(a_ref, b_ref, *refs):
    refs[-1][...] = a_ref[...] + b_ref[...]


def add_call(a, b, held):
    return pl.pallas_call(
        add_kernel,
        in_specs=[WHOLE] * (2 + len(held)),
        out_specs=WHOLE,
        out_shape=jax.ShapeDtypeStruct(a.shape, a.dtype),
        compiler_params=pltpu.CompilerParams(vmem_limit_bytes=24 * MIB),
        cost_estimate=cost(a.size, 12 * a.size),
        name="add_pieces",
    )(a, b, *(in_space(x, pltpu.VMEM) for x in held))


def join_kernel(a_ref, b_ref, *refs):
    half = a_ref.shape[0]
    refs[-1][:half, :] = a_ref[...]
    refs[-1][half:, :] = b_ref[...]


def join_call(a, b, held):
    rows, cols = a.shape
    return pl.pallas_call(
        join_kernel,
        in_specs=[WHOLE] * (2 + len(held)),
        out_specs=WHOLE,
        out_shape=jax.ShapeDtypeStruct((2 * rows, cols), a.dtype),
        compiler_params=pltpu.CompilerParams(vmem_limit_bytes=24 * MIB),
        cost_estimate=cost(a.size, 16 * a.size),
        name="join_pieces",
    )(a, b, *(in_space(x, pltpu.VMEM) for x in held))


def wide_sum(steps, keep, send, held):
    core, first, second, third = steps
    got = swap(send, "wide", core)
    for pairs in (first, second):
        h = keep.shape[0] // 2
        total = add_call(keep, got, held)
        send, keep = total[h:], total[:h]
        got = swap(send, "wide", pairs)
    mine = add_call(keep, got, held)
    mine = add_call(mine, swap(mine, "wide", third), held)
    for pairs in (second, first):
        mine = join_call(mine, swap(mine, "wide", pairs), held)
    return mine, swap(mine, "wide", core)


def per_device(narrow, wide, whole_rows, whole_cols, momentum, gradient, right_basis, signs, select):
    rows, cols = momentum.shape
    rank = right_basis.shape[1]
    fast = is_fast(narrow, wide)
    steps = exchanges(wide) if fast else None
    across = [(0, 1), (1, 0)]
    shi, slo, send, keep = left_call(fast, momentum, gradient, right_basis)
    sketch_rows = select.shape[0]
    scale = 1.0 / math.sqrt(sketch_rows)
    if fast:
        share = sketch_rows // wide
        first, second = wide_sum(steps, keep, send, (shi, slo))
        entries = entries_call(fast, select, share, signs, rows, (first,), (shi, slo))
        left, sketch = sketch_call(fast, first, second, entries, scale, (shi, slo))
        other = swap(sketch, "narrow", across)
        cut = cols // 256 * 128
        (right,) = right_call(left, shi, slo, 0, cut)
        pieces = [[right, swap(right, "narrow", across)]]
        right, sketch = right_call(left, shi, slo, cut, cols, sketch, other)
        pieces.append([right, swap(right, "narrow", across)])
        for pairs in reversed(steps[1:]):
            sketch = join_call(sketch, swap(sketch, "wide", pairs), ())
        sketches = (sketch, swap(sketch, "wide", steps[0]))
    else:
        first, second = lax.psum((keep, send), "wide")
        entries = entries_call(fast, select, sketch_rows, signs, rows, (), ())
        left, sketch = sketch_call(fast, first, second, entries, scale, ())
        sketch = lax.psum(sketch, "narrow")
        sketches = (sketch[: sketch_rows // 2], sketch[sketch_rows // 2 :])
        (right,) = right_call(left, shi, slo, 0, cols)
        pieces = [[lax.psum(right, "narrow")]]
    inv = factor_call(*sketches)
    left_terms, basis = basis_call(inv, left)
    left_terms, pieces[-1][-1] = lax.optimization_barrier((left_terms, pieces[-1][-1]))
    turned, right_terms, squares = rotate_call(inv, pieces)
    if fast:
        momentum_out = None
        for part, pairs in enumerate(steps):
            squares = add_call(squares, swap(squares, "wide", pairs), ())
            momentum_out = momentum_call(
                part, len(steps), shi, slo, left_terms, right_terms, momentum_out
            )
    else:
        squares = lax.psum(squares, "wide")
        momentum_out = momentum_call(0, 1, shi, slo, left_terms, right_terms)
    factor = math.sqrt(whole_rows * whole_cols / rank)
    update, basis_out = update_call(factor, turned, squares, basis, right_terms)
    return momentum_out, basis_out, update


def solution(mesh):
    in_specs = (P("narrow", "wide"), P("narrow", "wide"), P("wide", None), P(), P())
    out_specs = (P("narrow", "wide"), P("wide", None), P("narrow", "wide"))
    narrow, wide = mesh.shape["narrow"], mesh.shape["wide"]

    def whole(momentum, *rest):
        body = functools.partial(per_device, narrow, wide, *momentum.shape)
        return jax.shard_map(
            body, mesh=mesh, in_specs=in_specs, out_specs=out_specs, check_vma=False
        )(momentum, *rest)

    return whole
```

```python
import functools
import math

import jax
import jax.numpy as jnp
from jax import lax
from jax.experimental import pallas as pl
from jax.experimental.pallas import tpu as pltpu
from jax.sharding import PartitionSpec as P

decay_mu = 0.95
norm_epsilon = 1e-06

F32 = jnp.float32
BF16 = jnp.bfloat16
HIGH = lax.Precision.HIGHEST
MIB = 1024 * 1024
WHOLE = pl.BlockSpec(memory_space=pltpu.VMEM)


def split2(x):
    hi = x.astype(BF16)
    return hi, (x - hi.astype(F32)).astype(BF16)


def dot(a, b):
    return jnp.dot(a, b, preferred_element_type=F32)


in_space = pltpu.with_memory_space_constraint


def params(mib):
    return pltpu.CompilerParams(
        vmem_limit_bytes=mib * MIB, dimension_semantics=("arbitrary",)
    )


def cost(flops, bytes_accessed):
    return pl.CostEstimate(
        flops=int(flops), bytes_accessed=int(bytes_accessed), transcendentals=0
    )


TILE = 512
SLOTS = 2


def is_fast(narrow, wide):
    return narrow == 2 and wide == 16


def labels_of(fast):
    if not fast:
        return 0, 4
    index = lax.axis_index("wide")
    core, y, z = index & 1, (index >> 1) & 1, index >> 2
    za = (z >> 1) ^ (z & 1)
    even, odd = 2 * y + za, 4 + 2 * za + y
    return even + core * (odd - even), odd + core * (even - odd)


def left_kernel(
    fast,
    m_hbm,
    g_hbm,
    b_hbm,
    shi_ref,
    slo_ref,
    send_ref,
    keep_ref,
    m_ref,
    g_ref,
    b_ref,
    bhi,
    blo,
    lt,
    sems,
    b_sem,
):
    rows, cols = m_hbm.shape
    rank = b_ref.shape[1]
    block = rank // 8
    tiles = rows // TILE
    labels = labels_of(fast)

    def copies(t):
        source, slot = pl.ds(t * TILE, TILE), pl.ds(t % SLOTS * TILE, TILE)
        return (
            pltpu.make_async_copy(m_hbm.at[source], m_ref.at[slot], sems.at[0, t % SLOTS]),
            pltpu.make_async_copy(g_hbm.at[source], g_ref.at[slot], sems.at[1, t % SLOTS]),
        )

    b_copy = pltpu.make_async_copy(b_hbm, b_ref, b_sem)
    b_copy.start()
    for t in range(min(SLOTS - 1, tiles)):
        for copy in copies(t):
            copy.start()
    b_copy.wait()
    bhi[...], blo[...] = split2(b_ref[...])

    for t in range(tiles):
        for copy in copies(t):
            copy.wait()
        if t + SLOTS - 1 < tiles:
            for copy in copies(t + SLOTS - 1):
                copy.start()
        part, slot = slice(t * TILE, t * TILE + TILE), t % SLOTS * TILE
        slot = slice(slot, slot + TILE)
        hi, lo = split2(m_ref[slot, :] + g_ref[slot, :].astype(F32))
        shi_ref[part, :] = hi
        slo_ref[part, :] = lo
        both = dot(jnp.concatenate([hi, lo], axis=0), bhi[...])
        left = (both[:TILE] + both[TILE:]) + dot(hi, blo[...])
        lt[...] = left.T
        for side, ref in enumerate((keep_ref, send_ref)):
            for q in range(4):
                start = pl.multiple_of(block * (labels[side] ^ q), block)
                ref[block * q : block * q + block, part] = lt[pl.ds(start, block), :]


def left_call(fast, momentum, gradient, right_basis):
    rows, cols = momentum.shape
    rank = right_basis.shape[1]
    part = jax.ShapeDtypeStruct((rank // 2, rows), F32)
    hbm = pl.BlockSpec(memory_space=pltpu.HBM)
    return pl.pallas_call(
        functools.partial(left_kernel, fast),
        in_specs=[hbm] * 3,
        out_specs=[WHOLE] * 4,
        out_shape=[
            pltpu.VMEM((rows, cols), BF16),
            pltpu.VMEM((rows, cols), BF16),
            part,
            part,
        ],
        scratch_shapes=[
            pltpu.VMEM((SLOTS * TILE, cols), F32),
            pltpu.VMEM((SLOTS * TILE, cols), BF16),
            pltpu.VMEM((cols, rank), F32),
            pltpu.VMEM((cols, rank), BF16),
            pltpu.VMEM((cols, rank), BF16),
            pltpu.VMEM((rank, TILE), F32),
            pltpu.SemaphoreType.DMA((2, SLOTS)),
            pltpu.SemaphoreType.DMA,
        ],
        compiler_params=pltpu.CompilerParams(vmem_limit_bytes=24 * MIB),
        cost_estimate=cost(6 * rows * cols * rank, rows * cols * 6),
        name="left_factor",
    )(*(in_space(x, pltpu.HBM) for x in (momentum, gradient, right_basis)))


def entries_kernel(fast, select_ref, signs_ref, *refs):
    entries_ref, column_ref = refs[-2:]
    share, rows = entries_ref.shape
    column_ref[...] = jnp.broadcast_to(
        select_ref[...].astype(F32), (column_ref.shape[1], select_ref.shape[1])
    ).T
    start = pl.multiple_of(lax.axis_index("wide") * share, 8) if fast else 0
    select = column_ref[pl.ds(start, share), :1].astype(jnp.int32)
    first = pl.multiple_of(lax.axis_index("narrow") * rows, rows)
    column = first + lax.broadcasted_iota(jnp.int32, (1, rows), 1)
    bits = jnp.bitwise_and(select, column)
    for shift in (8, 4, 2, 1):
        bits = jnp.bitwise_xor(bits, jnp.right_shift(bits, shift))
    entries = (1 - 2 * jnp.bitwise_and(bits, 1)) * signs_ref[:, pl.ds(first, rows)]
    entries_ref[...] = entries.astype(F32).astype(BF16)


def entries_call(fast, select, share, signs, rows, after, held):
    return pl.pallas_call(
        functools.partial(entries_kernel, fast),
        in_specs=[WHOLE] * 2
        + [pl.BlockSpec(memory_space=pl.ANY)] * len(after)
        + [WHOLE] * len(held),
        out_specs=WHOLE,
        out_shape=jax.ShapeDtypeStruct((share, rows), BF16),
        scratch_shapes=[pltpu.VMEM((select.shape[0], 128), F32)],
        compiler_params=pltpu.CompilerParams(vmem_limit_bytes=24 * MIB),
        cost_estimate=cost(20 * share * rows, 2 * share * rows),
        name="hadamard_signs",
    )(
        select[None, :],
        signs[None, :],
        *after,
        *(in_space(x, pltpu.VMEM) for x in held),
    )


def sketch_kernel(fast, scale, a_ref, b_ref, entries_ref, *refs):
    left_ref, sketch_ref = refs[-2:]
    half, rows = a_ref.shape
    rank = 2 * half
    block = rank // 8
    labels = labels_of(fast)
    for side, ref in enumerate((a_ref, b_ref)):
        for q in range(4):
            start = pl.multiple_of(block * (labels[side] ^ q), block)
            hi, lo = split2(ref[block * q : block * q + block, :])
            left_ref[pl.ds(start, block), :] = hi
            left_ref[pl.ds(pl.multiple_of(rank + start, block), block), :] = lo
    both = lax.dot_general(
        entries_ref[...],
        left_ref[...],
        (((1,), (1,)), ((), ())),
        preferred_element_type=F32,
    )
    sketch_ref[...] = (both[:, :rank] + both[:, rank:]) * scale


def sketch_call(fast, first, second, entries, scale, held):
    half, rows = first.shape
    rank = 2 * half
    share = entries.shape[0]
    return pl.pallas_call(
        functools.partial(sketch_kernel, fast, scale),
        in_specs=[WHOLE] * (3 + len(held)),
        out_specs=[WHOLE] * 2,
        out_shape=[
            jax.ShapeDtypeStruct((2 * rank, rows), BF16),
            jax.ShapeDtypeStruct((share, rank), F32),
        ],
        compiler_params=pltpu.CompilerParams(vmem_limit_bytes=24 * MIB),
        cost_estimate=cost(4 * share * rank * rows, rows * rank * 8),
        name="sketch_rows",
    )(first, second, entries, *(in_space(x, pltpu.VMEM) for x in held))


def right_kernel(first, left_ref, shi_ref, slo_ref, *refs):
    if len(refs) > 1:
        mine_ref, other_ref, w_ref, sketch_ref = refs
        sketch_ref[...] = mine_ref[...] + other_ref[...]
    else:
        (w_ref,) = refs
    rank, cols = w_ref.shape
    for start in range(0, cols, 256):
        stop = min(start + 256, cols)
        source = slice(first + start, first + stop)
        both = dot(left_ref[...], shi_ref[:, source])
        last = dot(left_ref[:rank, :], slo_ref[:, source])
        w_ref[:, start:stop] = (both[:rank] + both[rank:]) + last


def right_call(left, shi, slo, first, stop, *sketches):
    rows = shi.shape[0]
    rank = left.shape[0] // 2
    cols = stop - first
    outs = [jax.ShapeDtypeStruct((rank, cols), F32)]
    if sketches:
        outs.append(jax.ShapeDtypeStruct(sketches[0].shape, F32))
    return pl.pallas_call(
        functools.partial(right_kernel, first),
        in_specs=[WHOLE] * (3 + len(sketches)),
        out_specs=[WHOLE] * len(outs),
        out_shape=outs,
        compiler_params=pltpu.CompilerParams(vmem_limit_bytes=24 * MIB),
        cost_estimate=cost(6 * rows * cols * rank, rows * cols * 4),
        name="right_factor",
    )(left, in_space(shi, pltpu.VMEM), in_space(slo, pltpu.VMEM), *sketches)


def eliminate(block):
    n = block.shape[0]
    groups = [block[8 * g : 8 * g + 8, :] for g in range(n // 8)]
    lane = lax.broadcasted_iota(jnp.int32, (8, n), 1)
    out = []
    for k in range(0, n, 4):
        g0, o = k // 8, k % 8
        rows = [groups[g0][o + j : o + j + 1, :] for j in range(4)]

        def entry(i, j):
            return jnp.broadcast_to(rows[i][:, k + j : k + j + 1], (8, n))

        u = [[entry(i, j) if j >= i else None for j in range(4)] for i in range(4)]
        inv = []
        low = [[None] * 4 for _ in range(4)]
        for i in range(4):
            inv.append(1.0 / u[i][i])
            for r in range(i + 1, 4):
                low[r][i] = u[i][r] * inv[i]
                for j in range(r, 4):
                    u[r][j] = u[r][j] - low[r][i] * u[i][j]
        inside = jnp.logical_and(lane >= k, lane < k + 4)
        q = []
        for i in range(4):
            base = jnp.where(inside, 0.0, jnp.broadcast_to(rows[i], (8, n)))
            base = jnp.where(lane == k + i, 1.0, base)
            for j in range(i):
                base = base - low[i][j] * q[j]
            q.append(base)
            out.append(jnp.where(lane <= k + i, base * lax.rsqrt(u[i][i]), 0.0)[:1])
        for g in range(g0 if o == 0 else g0 + 1, n // 8):
            x = groups[g]
            new = jnp.where(inside, 0.0, x)
            h = []
            for i in range(4):
                c = jnp.broadcast_to(x[:, k + i : k + i + 1], (8, n))
                for j in range(i):
                    c = c - h[j] * u[j][i]
                h.append(c * inv[i])
                new = new - h[i] * q[i]
            groups[g] = new
    return jnp.concatenate(out, axis=0)


def dot_high(a, b, dims=((1,), (0,))):
    return lax.dot_general(
        a, b, (dims, ((), ())), precision=HIGH, preferred_element_type=F32
    )


def factor_kernel(a_ref, b_ref, hi_ref, lo_ref):
    sketch = jnp.concatenate([a_ref[...], b_ref[...]], axis=0)
    gram = dot_high(sketch, sketch, ((0,), (0,)))
    half = gram.shape[0] // 2
    inv11 = eliminate(gram[:half, :half])
    l21 = dot_high(gram[half:, :half], inv11, ((1,), (1,)))
    inv22 = eliminate(gram[half:, half:] - dot_high(l21, l21, ((1,), (1,))))
    inv21 = -dot_high(inv22, dot_high(l21, inv11))
    top = jnp.concatenate([inv11, jnp.zeros_like(inv11)], axis=1)
    inverse = jnp.concatenate([top, jnp.concatenate([inv21, inv22], axis=1)], axis=0)
    hi_ref[...], lo_ref[...] = split2(inverse)


def factor_call(first, second):
    rank = first.shape[1]
    out = jax.ShapeDtypeStruct((rank, rank), BF16)
    return pl.pallas_call(
        factor_kernel,
        in_specs=[WHOLE] * 2,
        out_specs=[WHOLE] * 2,
        out_shape=[out, out],
        compiler_params=pltpu.CompilerParams(vmem_limit_bytes=24 * MIB),
        cost_estimate=cost(1e6, 1e5),
        name="factor_inverse",
    )(first, second)


def basis_kernel(hi_ref, lo_ref, raw_ref, terms_ref, basis_ref):
    rank = hi_ref.shape[0]
    hi, lo = raw_ref[:rank, :], raw_ref[rank:, :]
    basis = dot(hi_ref[...], hi) + (dot(hi_ref[...], lo) + dot(lo_ref[...], hi))
    basis = basis.T
    basis_ref[...] = basis
    hi, lo = split2(basis)
    terms_ref[...] = jnp.concatenate([hi, lo, hi], axis=1)


def basis_call(inv, raw):
    rows = raw.shape[1]
    rank = inv[0].shape[0]
    tile = 256
    inv_spec = pl.BlockSpec((rank, rank), lambda i: (0, 0))
    return pl.pallas_call(
        basis_kernel,
        grid=(rows // tile,),
        in_specs=[inv_spec] * 2 + [pl.BlockSpec((2 * rank, tile), lambda i: (0, i))],
        out_specs=[
            pl.BlockSpec((tile, 3 * rank), lambda i: (i, 0)),
            pl.BlockSpec((tile, rank), lambda i: (i, 0)),
        ],
        out_shape=[
            jax.ShapeDtypeStruct((rows, 3 * rank), BF16),
            jax.ShapeDtypeStruct((rows, rank), F32),
        ],
        compiler_params=params(24),
        cost_estimate=cost(1e6, 1e5),
        name="left_basis",
    )(*inv, raw)


def rotate_kernel(pieces, hi_ref, lo_ref, *refs):
    parts, (turned_ref, terms_ref, squares_ref) = refs[:-3], refs[-3:]
    rank = hi_ref.shape[0]
    squares = jnp.zeros((rank, 1), F32)
    start = 0
    for piece in pieces:
        total = piece[0]
        total = parts[total][...]
        for other in piece[1:]:
            total = total + parts[other][...]
        stop = start + total.shape[1]
        hi, lo = split2(total)
        right = dot(hi_ref[...], hi) + (dot(hi_ref[...], lo) + dot(lo_ref[...], hi))
        turned_ref[start:stop, :] = right.T
        hi, lo = split2((1.0 - decay_mu) * right)
        terms_ref[:rank, start:stop] = hi
        terms_ref[rank : 2 * rank, start:stop] = hi
        terms_ref[2 * rank :, start:stop] = lo
        squares = squares + jnp.sum(right * right, axis=1, keepdims=True)
        start = stop
    squares_ref[...] = jnp.broadcast_to(squares, (rank, 128)).T[:8, :]


def rotate_call(inv, pieces):
    rank = inv[0].shape[0]
    cols = sum(piece[0].shape[1] for piece in pieces)
    flat, places = [], []
    for piece in pieces:
        places.append(tuple(range(len(flat), len(flat) + len(piece))))
        flat.extend(piece)
    return pl.pallas_call(
        functools.partial(rotate_kernel, tuple(places)),
        in_specs=[WHOLE] * (2 + len(flat)),
        out_specs=[WHOLE] * 3,
        out_shape=[
            jax.ShapeDtypeStruct((cols, rank), F32),
            jax.ShapeDtypeStruct((3 * rank, cols), BF16),
            jax.ShapeDtypeStruct((8, rank), F32),
        ],
        compiler_params=pltpu.CompilerParams(vmem_limit_bytes=24 * MIB),
        cost_estimate=cost(6 * cols * rank * rank, cols * rank * 16),
        name="right_rotate",
    )(*inv, *flat)


def momentum_kernel(first, shi_ref, slo_ref, left_ref, terms_ref, *refs):
    out_ref = refs[-1]
    tile = out_ref.shape[0]
    rows = pl.ds(pl.multiple_of((first + pl.program_id(0)) * tile, tile), tile)
    summed = shi_ref[rows, :].astype(F32) + slo_ref[rows, :].astype(F32)
    out_ref[...] = summed - dot(left_ref[rows, :], terms_ref[...])


def momentum_call(part, parts, shi, slo, left, terms, before=None):
    rows, cols = shi.shape
    rank = left.shape[1] // 3
    tile = 256
    count = max(rows // tile // parts, 1)
    first = part * count
    operands = [in_space(shi, pltpu.VMEM), in_space(slo, pltpu.VMEM), left, terms]
    specs = [WHOLE] * 4
    if before is not None:
        operands.append(before)
        specs.append(pl.BlockSpec(memory_space=pl.ANY))
    return pl.pallas_call(
        functools.partial(momentum_kernel, first),
        grid=(count,),
        in_specs=specs,
        out_specs=pl.BlockSpec((tile, cols), lambda i: (first + i, 0)),
        out_shape=jax.ShapeDtypeStruct((rows, cols), F32),
        input_output_aliases={} if before is None else {4: 0},
        compiler_params=params(24),
        cost_estimate=cost(6 * rows * cols * rank // parts, rows * cols * 4 // parts),
        name="momentum_update",
    )(*operands)


def update_kernel(factor, turned_ref, squares_ref, left_ref, terms_ref, update_ref, basis_ref):
    norms = jnp.sqrt(squares_ref[:1, :] + norm_epsilon)
    tile = update_ref.shape[0]
    step = pl.program_id(0)
    rows = pl.ds(pl.multiple_of(step * tile, tile), tile)
    hi, lo = split2(left_ref[rows, :] * (factor / norms))
    scaled = jnp.concatenate([hi, lo, hi], axis=1)
    update_ref[...] = dot(scaled, terms_ref[...]).astype(BF16)
    share = basis_ref.shape[0]
    part = pl.ds(pl.multiple_of(step * share, 8), share)
    basis_ref[...] = turned_ref[part, :] * (1.0 / norms)


def update_call(factor, turned, squares, left, terms):
    cols, rank = turned.shape
    rows = left.shape[0]
    tile = min(rows, 512)
    share = cols // (rows // tile)
    return pl.pallas_call(
        functools.partial(update_kernel, factor / (1.0 - decay_mu)),
        grid=(rows // tile,),
        in_specs=[WHOLE] * 4,
        out_specs=[
            pl.BlockSpec((tile, cols), lambda i: (i, 0)),
            pl.BlockSpec((share, rank), lambda i: (i, 0)),
        ],
        out_shape=[
            jax.ShapeDtypeStruct((rows, cols), BF16),
            jax.ShapeDtypeStruct((cols, rank), F32),
        ],
        compiler_params=params(24),
        cost_estimate=cost(6 * rows * cols * rank, rows * cols * 2),
        name="update_basis",
    )(turned, squares, left, terms)


def swap(x, axis, pairs):
    return lax.ppermute(x, axis, pairs)


def exchanges(wide):
    core, y, za, zb = 1, 2, 4, 12
    steps = ((core, core), (y, za), (za, y), (zb, zb))
    return [[(i, i ^ bits[i % 2]) for i in range(wide)] for bits in steps]


def add_kernel(a_ref, b_ref, *refs):
    refs[-1][...] = a_ref[...] + b_ref[...]


def add_call(a, b, held):
    return pl.pallas_call(
        add_kernel,
        in_specs=[WHOLE] * (2 + len(held)),
        out_specs=WHOLE,
        out_shape=jax.ShapeDtypeStruct(a.shape, a.dtype),
        compiler_params=pltpu.CompilerParams(vmem_limit_bytes=24 * MIB),
        cost_estimate=cost(a.size, 12 * a.size),
        name="add_pieces",
    )(a, b, *(in_space(x, pltpu.VMEM) for x in held))


def halves_kernel(a_ref, b_ref, *refs):
    send_ref, keep_ref = refs[-2:]
    h = send_ref.shape[0]
    send_ref[...] = a_ref[h:, :] + b_ref[h:, :]
    keep_ref[...] = a_ref[:h, :] + b_ref[:h, :]


def halves_call(a, b, held):
    half = jax.ShapeDtypeStruct((a.shape[0] // 2, a.shape[1]), a.dtype)
    return pl.pallas_call(
        halves_kernel,
        in_specs=[WHOLE] * (2 + len(held)),
        out_specs=[WHOLE] * 2,
        out_shape=[half, half],
        compiler_params=pltpu.CompilerParams(vmem_limit_bytes=24 * MIB),
        cost_estimate=cost(a.size, 12 * a.size),
        name="add_halves",
    )(a, b, *(in_space(x, pltpu.VMEM) for x in held))


def join_kernel(a_ref, b_ref, *refs):
    half = a_ref.shape[0]
    refs[-1][:half, :] = a_ref[...]
    refs[-1][half:, :] = b_ref[...]


def join_call(a, b, held):
    rows, cols = a.shape
    return pl.pallas_call(
        join_kernel,
        in_specs=[WHOLE] * (2 + len(held)),
        out_specs=WHOLE,
        out_shape=jax.ShapeDtypeStruct((2 * rows, cols), a.dtype),
        compiler_params=pltpu.CompilerParams(vmem_limit_bytes=24 * MIB),
        cost_estimate=cost(a.size, 16 * a.size),
        name="join_pieces",
    )(a, b, *(in_space(x, pltpu.VMEM) for x in held))


def wide_sum(steps, keep, send, held):
    core, first, second, third = steps
    got = swap(send, "wide", core)
    for pairs in (first, second):
        send, keep = halves_call(keep, got, held)
        got = swap(send, "wide", pairs)
    mine = add_call(keep, got, held)
    mine = add_call(mine, swap(mine, "wide", third), held)
    for pairs in (second, first):
        mine = join_call(mine, swap(mine, "wide", pairs), held)
    return mine, swap(mine, "wide", core)


def per_device(narrow, wide, whole_rows, whole_cols, momentum, gradient, right_basis, signs, select):
    rows, cols = momentum.shape
    rank = right_basis.shape[1]
    fast = is_fast(narrow, wide)
    steps = exchanges(wide) if fast else None
    across = [(0, 1), (1, 0)]
    shi, slo, send, keep = left_call(fast, momentum, gradient, right_basis)
    sketch_rows = select.shape[0]
    scale = 1.0 / math.sqrt(sketch_rows)
    if fast:
        share = sketch_rows // wide
        first, second = wide_sum(steps, keep, send, (shi, slo))
        entries = entries_call(fast, select, share, signs, rows, (first,), (shi, slo))
        left, sketch = sketch_call(fast, first, second, entries, scale, (shi, slo))
        other = swap(sketch, "narrow", across)
        cut = cols // 256 * 128
        (right,) = right_call(left, shi, slo, 0, cut)
        pieces = [[right, swap(right, "narrow", across)]]
        right, sketch = right_call(left, shi, slo, cut, cols, sketch, other)
        pieces.append([right, swap(right, "narrow", across)])
        for pairs in reversed(steps[1:]):
            sketch = join_call(sketch, swap(sketch, "wide", pairs), ())
        sketches = (sketch, swap(sketch, "wide", steps[0]))
    else:
        first, second = lax.psum((keep, send), "wide")
        entries = entries_call(fast, select, sketch_rows, signs, rows, (), ())
        left, sketch = sketch_call(fast, first, second, entries, scale, ())
        sketch = lax.psum(sketch, "narrow")
        sketches = (sketch[: sketch_rows // 2], sketch[sketch_rows // 2 :])
        (right,) = right_call(left, shi, slo, 0, cols)
        pieces = [[lax.psum(right, "narrow")]]
    inv = factor_call(*sketches)
    left_terms, basis = basis_call(inv, left)
    left_terms, pieces[-1][-1] = lax.optimization_barrier((left_terms, pieces[-1][-1]))
    turned, right_terms, squares = rotate_call(inv, pieces)
    if fast:
        momentum_out = None
        for part, pairs in enumerate(steps):
            squares = add_call(squares, swap(squares, "wide", pairs), ())
            momentum_out = momentum_call(
                part, len(steps), shi, slo, left_terms, right_terms, momentum_out
            )
    else:
        squares = lax.psum(squares, "wide")
        momentum_out = momentum_call(0, 1, shi, slo, left_terms, right_terms)
    factor = math.sqrt(whole_rows * whole_cols / rank)
    update, basis_out = update_call(factor, turned, squares, basis, right_terms)
    return momentum_out, basis_out, update


def solution(mesh):
    in_specs = (P("narrow", "wide"), P("narrow", "wide"), P("wide", None), P(), P())
    out_specs = (P("narrow", "wide"), P("wide", None), P("narrow", "wide"))
    narrow, wide = mesh.shape["narrow"], mesh.shape["wide"]

    def whole(momentum, *rest):
        body = functools.partial(per_device, narrow, wide, *momentum.shape)
        return jax.shard_map(
            body, mesh=mesh, in_specs=in_specs, out_specs=out_specs, check_vma=False
        )(momentum, *rest)

    return whole
```
